32 devices in a mesh: group: 8 (over y, x, core), member: 4 (over z).
Axes of the slice: x: 2, y: 2, z: 4, core: 2. Of those that a mesh axis runs over, the one named last changes fastest.
Arguments:
- spectra: bfloat16 [1024, 8, 2048], P(('group', 'member'))
- partner: int32 [8], replicated, may hold values from 0 to 7, as said below
Outputs:
- correlations: bfloat16 [1024, 128, 128], P(('group', 'member'))
The draws below stay inside these ranges and needn't reach their ends.
Inputs may be any that keep to these rules, and one draw needn't show every extreme that they name: partner is one round of a round-robin among the 8 groups: partner[partner[g]] == g and partner[g] != g for every g.
All inputs are finite; a program needn't handle non-finite values.
Results may differ from the reference program's by a relative error of at most 0.007.
Values may be sent and summed in bfloat16 or wider, within the bound.
No kernel may reach another device: no remote copies, remote signals or barrier semaphores. Data moves between devices by JAX's collectives and lax.ppermute only.
A program may use at most 192 MiB of HBM per device.

```python
import math
import jax
import jax.numpy as jnp
from jax import lax

CH_DEV = 32
WINDOWS = 8
FREQS = 1024
LAGS = 128
HALF = 64
GROUP_CH = 128
CHANNELS = 1024
N_GROUP = 8
N_MEMBER = 4


def draw_spectra(key, part):
    keys = jax.random.split(key, 6)
    positions = jnp.arange(FREQS).astype(jnp.float32)
    spread_top = math.log(10.0)
    channel_gain = jnp.exp(jax.random.uniform(keys[0], (CHANNELS, 1, 1), jnp.float32, 0.0, spread_top))
    window_gain = jnp.exp(jax.random.uniform(keys[1], (CHANNELS, WINDOWS, 1), jnp.float32, 0.0, math.log(3.0)))
    tilt = jax.random.uniform(keys[2], (CHANNELS, 1, 1), jnp.float32, 1.0, 4.0)
    phase = jax.random.uniform(keys[3], (CHANNELS, 1, 1), jnp.float32, 0.0, 2.0 * math.pi)
    shape_gain = jnp.exp(0.5 * math.log(10.0) * (1.0 + jnp.sin(2.0 * math.pi * tilt * positions / FREQS + phase)))
    rough = jax.random.uniform(keys[4], (CHANNELS, WINDOWS, FREQS), jnp.float32, 0.5, 1.5)
    amplitude = channel_gain * window_gain * shape_gain * rough
    noise = jax.random.normal(keys[5], (CHANNELS, WINDOWS, 2, FREQS), jnp.float32)
    values = noise * amplitude[:, :, None, :]
    return values.reshape(CHANNELS, WINDOWS, 2 * FREQS).astype(jnp.bfloat16)


def draw_partner(key, part):
    round_key = jax.random.fold_in(key, 11)
    label_key = jax.random.fold_in(key, 23)
    group_count = N_GROUP
    odd_count = group_count - 1
    round_index = jax.random.randint(round_key, (), 0, odd_count, dtype=jnp.int32)
    positions = jnp.arange(group_count, dtype=jnp.int32)
    paired = jnp.mod(round_index - positions, odd_count)
    paired = jnp.where(paired == positions, odd_count, paired)
    last_pair = jnp.mod(round_index * (group_count // 2), odd_count)
    base = jnp.where(positions == odd_count, last_pair, paired).astype(jnp.int32)
    labels = jax.random.permutation(label_key, group_count).astype(jnp.int32)
    inverse = jnp.argsort(labels, stable=True).astype(jnp.int32)
    return labels[base[inverse]].astype(jnp.int32)


def setup_inputs(seed: int = 0) -> dict:
    key_of = jax.random.split(jax.random.key(seed), 3)
    spectra = draw_spectra(jax.random.fold_in(key_of[2], 71), 0)
    partner = draw_partner(jax.random.fold_in(key_of[2], 71), 0)
    return {"spectra": spectra, "partner": partner}


def band_matrix(freq_count):
    positions = jnp.arange(freq_count, dtype=jnp.int32)
    distance = jnp.abs(positions[:, None] - positions[None, :])
    band_ones = (distance <= HALF).astype(jnp.float32)
    counts = (jnp.minimum(positions + HALF, freq_count - 1) - jnp.maximum(positions - HALF, 0) + 1).astype(jnp.float32)
    return (band_ones, counts)

def whiten(spectra):
    freq_count = spectra.shape[2] // 2
    window_count = spectra.shape[1]
    real_part = spectra[:, :, :freq_count].astype(jnp.float32)
    imag_part = spectra[:, :, freq_count:].astype(jnp.float32)
    power_sum = lax.optimization_barrier(jnp.sum(real_part * real_part + imag_part * imag_part, axis=1))
    band_ones, counts = band_matrix(freq_count)
    smoothed = jnp.dot(power_sum, band_ones, precision=lax.Precision.HIGHEST)
    average = smoothed / (counts * window_count)
    inverse_amp = 1.0 / jnp.sqrt(average + 1e-05)
    factor = jnp.concatenate([inverse_amp, inverse_amp], axis=1)
    return (spectra.astype(jnp.float32) * factor[:, None, :]).astype(jnp.bfloat16)

def lag_matrix(freq_count, window_count):
    lag_values = jnp.arange(LAGS, dtype=jnp.int32) - LAGS // 2
    freq_values = jnp.arange(freq_count, dtype=jnp.int32)
    residue = jnp.mod(freq_values[:, None] * lag_values[None, :], 2 * freq_count)
    angles = jnp.pi * residue.astype(jnp.float32) / freq_count
    norm_factor = 1.0 / math.sqrt(window_count * freq_count)
    return jnp.concatenate([jnp.cos(angles) * norm_factor, -jnp.sin(angles) * norm_factor], axis=0).astype(jnp.bfloat16)

def correlate(own_rows, other_rows, lag_table):
    freq_count = own_rows.shape[2] // 2
    own_real = own_rows[:, :, :freq_count].astype(jnp.float32)
    own_imag = own_rows[:, :, freq_count:].astype(jnp.float32)
    other_real = other_rows[:, :, :freq_count].astype(jnp.float32)
    other_imag = other_rows[:, :, freq_count:].astype(jnp.float32)
    left_real = jnp.concatenate([own_real, own_imag], axis=1)
    left_imag = jnp.concatenate([own_imag, -own_real], axis=1)
    right_part = jnp.concatenate([other_real, other_imag], axis=1)
    cross_real = jnp.einsum('awf,bwf->abf', left_real, right_part, precision=lax.Precision.HIGHEST)
    cross_imag = jnp.einsum('awf,bwf->abf', left_imag, right_part, precision=lax.Precision.HIGHEST)
    cross = jnp.concatenate([cross_real, cross_imag], axis=2).astype(jnp.bfloat16)
    own_count = own_rows.shape[0]
    other_count = other_rows.shape[0]
    lagged = jnp.dot(cross.reshape(own_count * other_count, 2 * freq_count), lag_table, preferred_element_type=jnp.float32)
    return lagged.reshape(own_count, other_count, lag_table.shape[1])

def reference(spectra, partner):
    whitened = whiten(spectra)
    lag_table = lag_matrix(FREQS, WINDOWS)
    block_total = CHANNELS // CH_DEV

    def one_block(block_index):
        group_index = block_index // N_MEMBER
        partner_group = partner[group_index]
        own_rows = lax.dynamic_slice_in_dim(whitened, (block_index * CH_DEV).astype(jnp.int32), CH_DEV, 0)
        other_rows = lax.dynamic_slice_in_dim(whitened, (partner_group * GROUP_CH).astype(jnp.int32), GROUP_CH, 0)
        return correlate(own_rows, other_rows, lag_table).astype(jnp.bfloat16)
    stacked = lax.map(one_block, jnp.arange(block_total, dtype=jnp.int32))
    return stacked.reshape(CHANNELS, GROUP_CH, LAGS)
```

```python
import itertools
import math

import jax
import jax.numpy as jnp
import ml_dtypes
import numpy as np
from jax import lax
from jax.experimental import pallas as pl
from jax.experimental.pallas import tpu as pltpu
from jax.sharding import PartitionSpec as P

LAGS = 128
HALF = 64
FINE = 16
ROWS = 16
VMEM_BYTES = 48 * 1024 * 1024


def lag_rows(freq_count, window_count):
    lag = np.arange(LAGS) - LAGS // 2
    freq = np.arange(freq_count)
    angle = np.pi * np.mod(lag[:, None] * freq[None, :], 2 * freq_count) / freq_count
    norm = 1.0 / math.sqrt(window_count * freq_count)
    rows = np.concatenate([np.cos(angle), -np.sin(angle)], axis=0) * norm
    return rows.astype(np.float32).astype(ml_dtypes.bfloat16)


def whiten_block(raw_ref, out_ref, wide_ref):
    rows, windows, width = raw_ref.shape
    freqs = width // 2
    lanes = windows * FINE
    groups = freqs // lanes
    for slab in range(2 * groups):
        value = raw_ref[:, :, slab * lanes : (slab + 1) * lanes].astype(jnp.float32)
        wide_ref[slab] = value.reshape(rows * windows, lanes)

    def window(slab, w):
        return wide_ref[slab, pl.ds(w, rows, stride=windows), :]

    pieces = []
    for group in range(groups):
        piece = jnp.zeros((rows, lanes), jnp.float32)
        for w in range(windows):
            real, imag = window(group, w), window(groups + group, w)
            piece += real * real + imag * imag
        pieces.append(piece)
    power = jnp.concatenate(pieces, axis=1)
    edge = jnp.zeros((rows, 2 * HALF), jnp.float32)
    padded = jnp.concatenate([edge, power, edge], axis=1)
    total = padded
    length = padded.shape[1]
    step = 1
    while step < 2 * HALF:
        total = total + pltpu.roll(total, length - step, axis=1)
        step *= 2
    total = total + pltpu.roll(padded, length - 2 * HALF, axis=1)
    smoothed = pltpu.roll(total, length - HALF, axis=1)[:, :freqs]
    place = lax.broadcasted_iota(jnp.int32, (rows, freqs), 1)
    counts = jnp.minimum(place + HALF, freqs - 1) - jnp.maximum(place - HALF, 0) + 1
    average = smoothed / (counts.astype(jnp.float32) * windows)
    factor = 1.0 / jnp.sqrt(average + 1e-05)
    granule = lax.broadcasted_iota(jnp.int32, (rows, lanes), 1) // FINE
    for part in range(2):
        for group in range(groups):
            scale = factor[:, group * lanes : (group + 1) * lanes]
            items = [window(part * groups + group, w) * scale for w in range(windows)]
            dist = windows // 2
            while dist:
                keep = (granule & dist) == 0
                nxt = list(items)
                for i in range(windows):
                    if i & dist:
                        continue
                    j = i + dist
                    nxt[i] = jnp.where(keep, items[i], pltpu.roll(items[j], dist * FINE, axis=1))
                    nxt[j] = jnp.where(keep, pltpu.roll(items[i], lanes - dist * FINE, axis=1), items[j])
                items = nxt
                dist //= 2
            for i in range(windows):
                out_ref[group * windows + i, :, part * lanes : (part + 1) * lanes] = items[i].astype(jnp.bfloat16)


def whiten(raw):
    channels, windows, width = raw.shape
    blocks = width // 2 // FINE
    return pl.pallas_call(
        whiten_block,
        grid=(channels // ROWS,),
        in_specs=[pl.BlockSpec((ROWS, windows, width), lambda i: (i, 0, 0))],
        out_specs=pl.BlockSpec((blocks, ROWS, 2 * windows * FINE), lambda i: (0, i, 0)),
        out_shape=jax.ShapeDtypeStruct((blocks, channels, 2 * windows * FINE), jnp.bfloat16),
        scratch_shapes=[pltpu.VMEM((blocks // windows * 2, ROWS * windows, windows * FINE), jnp.float32)],
        compiler_params=pltpu.CompilerParams(vmem_limit_bytes=VMEM_BYTES),
        name="whiten",
    )(raw)


def correlate_kernel(order_ref, a1, a2, b1, b2, b3, b4, table_ref, own_ref, other_ref, rows_ref, rhs_ref, cross_ref, flip_ref):
    step = pl.program_id(1)
    chunk, _, depth = a1.shape
    half = depth // 2
    a_count = 2 * ROWS
    b_count = 4 * ROWS
    width = 2 * b_count
    swap_a, swap_b, first_half = order_ref[0], order_ref[1], order_ref[2]
    fine_row = lax.broadcasted_iota(jnp.int32, (FINE, depth), 0)
    fine_lane = lax.broadcasted_iota(jnp.int32, (FINE, depth), 1) % FINE
    mask = (fine_row == fine_lane).astype(jnp.float32)

    def one_block(f, carry):
        for index, ref in enumerate((a1, a2)):
            at = pl.multiple_of((index ^ swap_a) * ROWS, ROWS)
            rows_ref[pl.ds(at, ROWS), :] = ref[f].astype(jnp.float32)
        for index, ref in enumerate((b1, b2, b3, b4)):
            spot = ((index // 2) ^ swap_b) * 2 + ((index % 2) ^ first_half)
            at = pl.multiple_of(spot * ROWS, ROWS)
            value = ref[f]
            rhs_ref[pl.ds(at, ROWS), :] = value
            rhs_ref[pl.ds(b_count + at, ROWS), :half] = -value[:, half:]
            rhs_ref[pl.ds(b_count + at, ROWS), half:] = value[:, :half]
        parts = []
        for i in range(a_count):
            row = jnp.broadcast_to(rows_ref[i : i + 1, :], (FINE, depth))
            parts.append((row * mask).astype(jnp.bfloat16))
        left = jnp.concatenate(parts, axis=0)
        cross = lax.dot_general(
            left, rhs_ref[...], (((1,), (1,)), ((), ())), preferred_element_type=jnp.float32
        ).astype(jnp.bfloat16)
        at = pl.multiple_of((step * chunk + f) * FINE, FINE)
        for i in range(a_count):
            cross_ref[pl.ds(at, FINE), i * width : (i + 1) * width] = cross[i * FINE : (i + 1) * FINE]
        return carry

    lax.fori_loop(0, chunk, one_block, 0)

    @pl.when(step == pl.num_programs(1) - 1)
    def _():
        low = lax.broadcasted_iota(jnp.int32, (LAGS, width), 1) < b_count
        for i in range(a_count):
            both = jnp.dot(
                table_ref[...], cross_ref[:, i * width : (i + 1) * width], preferred_element_type=jnp.float32
            )
            cos_part, sin_part = both[:LAGS], both[LAGS:]
            joined = jnp.where(
                low,
                cos_part + pltpu.roll(sin_part, b_count, axis=1),
                pltpu.roll(cos_part, b_count, axis=1) - sin_part,
            )
            turned = joined.T
            own_ref[(i // ROWS) ^ swap_a, i % ROWS] = turned[:b_count].astype(jnp.bfloat16)
            flip_ref[pl.ds(i, b_count, stride=a_count), :] = turned[b_count:]
        span = b_count // 2 * a_count
        for index in range(2):
            value = flip_ref[index * span : (index + 1) * span, :].astype(jnp.bfloat16)
            other_ref[index ^ swap_b] = value.reshape(b_count // 2, a_count, LAGS)


def correlate(order, a_list, b_list, table, b_blocks, chunk=8):
    blocks, _, depth = a_list[0][0].shape
    freqs = blocks * FINE
    a_count, b_count = 2 * ROWS, 4 * ROWS
    width = 2 * b_count
    stride = 4 if b_blocks > 1 else 0

    def spec(offset, advance):
        return pl.BlockSpec((chunk, ROWS, depth), lambda j, s, *_: (s, offset + advance * j, 0))

    return pl.pallas_call(
        correlate_kernel,
        grid_spec=pltpu.PrefetchScalarGridSpec(
            num_scalar_prefetch=1,
            grid=(b_blocks, blocks // chunk),
            in_specs=[spec(o, 0) for _, o in a_list]
            + [spec(o, stride) for _, o in b_list]
            + [pl.BlockSpec((2 * LAGS, freqs), lambda j, s, *_: (0, 0))],
            out_specs=[
                pl.BlockSpec((2, ROWS, b_count, LAGS), lambda j, s, *_: (0, 0, j, 0)),
                pl.BlockSpec((2, b_count // 2, a_count, LAGS), lambda j, s, *_: (0, j, 0, 0)),
            ],
            scratch_shapes=[
                pltpu.VMEM((a_count, depth), jnp.float32),
                pltpu.VMEM((width, depth), jnp.bfloat16),
                pltpu.VMEM((freqs, a_count * width), jnp.bfloat16),
                pltpu.VMEM((b_count * a_count, LAGS), jnp.float32),
            ],
        ),
        out_shape=[
            jax.ShapeDtypeStruct((2, ROWS, b_blocks * b_count, LAGS), jnp.bfloat16),
            jax.ShapeDtypeStruct((2, b_blocks * b_count // 2, a_count, LAGS), jnp.bfloat16),
        ],
        compiler_params=pltpu.CompilerParams(
            vmem_limit_bytes=VMEM_BYTES, dimension_semantics=("arbitrary", "arbitrary")
        ),
        name="correlate",
    )(order, *[a for a, _ in a_list], *[b for b, _ in b_list], table)


def whiten_half(raw, which):
    channels, windows, width = raw.shape
    blocks = width // 2 // FINE
    depth = 2 * windows * FINE

    def kernel(which_ref, raw_ref, out_ref, wide_ref):
        whiten_block(raw_ref, out_ref, wide_ref)

    return pl.pallas_call(
        kernel,
        grid_spec=pltpu.PrefetchScalarGridSpec(
            num_scalar_prefetch=1,
            grid=(1,),
            in_specs=[pl.BlockSpec((ROWS, windows, width), lambda i, which_ref: (which_ref[0], 0, 0))],
            out_specs=pl.BlockSpec((blocks, ROWS, depth), lambda i, *_: (0, 0, 0)),
            scratch_shapes=[pltpu.VMEM((blocks // windows * 2, ROWS * windows, windows * FINE), jnp.float32)],
        ),
        out_shape=jax.ShapeDtypeStruct((blocks, ROWS, depth), jnp.bfloat16),
        compiler_params=pltpu.CompilerParams(vmem_limit_bytes=VMEM_BYTES),
        name="whiten_half",
    )(which, raw)


def whiten_sorted(raw, own, stays):
    rows, windows, width = raw.shape
    blocks, _, depth = own.shape

    def kernel(stays_ref, raw_ref, own_ref, stay_ref, move_ref, new_ref, wide_ref):
        whiten_block(raw_ref, new_ref, wide_ref)

        @pl.when(stays_ref[0] == 1)
        def _():
            stay_ref[...] = own_ref[...]
            move_ref[...] = new_ref[...]

        @pl.when(stays_ref[0] != 1)
        def _():
            stay_ref[...] = new_ref[...]
            move_ref[...] = own_ref[...]

    shape = jax.ShapeDtypeStruct(own.shape, jnp.bfloat16)
    return pl.pallas_call(
        kernel,
        in_specs=[
            pl.BlockSpec(memory_space=pltpu.SMEM),
            pl.BlockSpec(memory_space=pltpu.VMEM),
            pl.BlockSpec(memory_space=pltpu.VMEM),
        ],
        out_specs=[pl.BlockSpec(memory_space=pltpu.VMEM)] * 2,
        out_shape=[shape, shape],
        scratch_shapes=[
            pltpu.VMEM(own.shape, jnp.bfloat16),
            pltpu.VMEM((blocks // windows * 2, ROWS * windows, windows * FINE), jnp.float32),
        ],
        compiler_params=pltpu.CompilerParams(vmem_limit_bytes=VMEM_BYTES),
        name="whiten_sorted",
    )(stays, raw, own)


def assign_roles(partner):
    count = partner.shape[0]
    chips = count // 2

    def kernel(partner_ref, out_ref):
        for group in range(count):
            out_ref[group] = -1
        for group in range(count):

            @pl.when(out_ref[group] < 0)
            def _():
                def walk(_, here):
                    there = partner_ref[here]
                    out_ref[here] = 0
                    out_ref[there] = 1
                    return there ^ 1

                lax.fori_loop(0, chips, walk, jnp.int32(group))

        target = [partner_ref[2 * chip + 1 - out_ref[2 * chip]] // 2 for chip in range(chips)]
        rank = jnp.int32(0)
        for i in range(chips):
            for j in range(i + 1, chips):
                rank += jnp.where(target[j] < target[i], math.factorial(chips - 1 - i), 0)
        out_ref[count] = rank

    return pl.pallas_call(
        kernel,
        in_specs=[pl.BlockSpec(memory_space=pltpu.SMEM)],
        out_specs=pl.BlockSpec(memory_space=pltpu.SMEM),
        out_shape=jax.ShapeDtypeStruct((count + 1,), jnp.int32),
        name="assign_roles",
    )(partner)


def permute(value, groups, members, target):
    pairs = []
    for group, member in itertools.product(range(groups), range(members)):
        to_group, to_member = target(group, member)
        pairs.append((group * members + member, to_group * members + to_member))
    return lax.ppermute(value, ("group", "member"), pairs)


def on_device_any(spectra, partner):
    group_count = lax.axis_size("group")
    channels, windows, width = spectra.shape
    white = whiten(spectra)
    blocks, _, depth = white.shape
    spread = lax.all_to_all(white, "group", split_axis=1, concat_axis=1, tiled=True)
    shares = spread.reshape(blocks, group_count, channels // group_count, depth)
    ordered = jnp.take(shares, partner, axis=1).reshape(white.shape)
    arrived = lax.all_to_all(ordered, "group", split_axis=1, concat_axis=1, tiled=True)
    theirs = lax.all_gather(arrived, "member", axis=1, tiled=True)
    table = jnp.asarray(lag_rows(width // 2, windows))
    others = theirs.shape[1]
    order = jnp.zeros((3,), jnp.int32)
    result, _ = correlate(
        order, [(white, 0), (white, 1)], [(theirs, q) for q in range(4)], table, others // (4 * ROWS)
    )
    return result.reshape(channels, others, LAGS)


def on_device_pairs(spectra, partner):
    groups, members = lax.axis_size("group"), lax.axis_size("member")
    chips = groups // 2
    channels, windows, width = spectra.shape
    group, member = lax.axis_index("group"), lax.axis_index("member")
    core = group % 2

    def across(value):
        return permute(value, groups, members, lambda g, m: (g ^ 1, m))

    roles = assign_roles(partner)
    rank = roles[groups]
    stays = 1 - lax.dynamic_slice_in_dim(roles, group, 1)
    received = across(lax.dynamic_slice_in_dim(spectra, (1 - core) * ROWS, ROWS, 0))
    own = whiten_half(spectra, core.reshape(1))
    stay, move = whiten_sorted(received, own, stays)

    far = (2, 0, 3, 1)
    back = tuple(far.index(m) for m in range(members))
    near = (0, 2, 1, 3)
    first = permute(stay, groups, members, lambda g, m: (g, far[m]))
    second = permute(stay, groups, members, lambda g, m: (g, near[m]))

    orders = list(itertools.permutations(range(chips)))

    def go(order):
        def branch(value):
            same = permute(value, groups, members, lambda g, m: (2 * order[g // 2] + g % 2, m))
            other = permute(value, groups, members, lambda g, m: (2 * order[g // 2] + g % 2, m ^ 1))
            return same, other

        return branch

    def home(order):
        def branch(same, other):
            same = permute(same, groups, members, lambda g, m: (2 * order.index(g // 2) + g % 2, m))
            other = permute(other, groups, members, lambda g, m: (2 * order.index(g // 2) + g % 2, m ^ 1))
            return same, other

        return branch

    here, there = lax.switch(rank, [go(order) for order in orders], move)
    table = jnp.asarray(lag_rows(width // 2, windows))
    order = jnp.stack([(member < 2).astype(jnp.int32), member % 2, core])
    straight, mirrored = correlate(
        order,
        [(first, 0), (second, 0)],
        [(here, 0), (across(here), 0), (there, 0), (across(there), 0)],
        table,
        1,
    )
    from_far = permute(straight[0], groups, members, lambda g, m: (g, back[m]))
    from_near = permute(straight[1], groups, members, lambda g, m: (g, near[m]))
    here, there = lax.switch(rank, [home(order) for order in orders], mirrored[0], mirrored[1])

    even = member % 2 == 0
    left, right = jnp.where(even, from_near, from_far), jnp.where(even, from_far, from_near)
    stay_part = jnp.concatenate([left, right], axis=1).reshape(-1, LAGS)
    left, right = jnp.where(even, here, there), jnp.where(even, there, here)
    move_part = jnp.concatenate([left, right], axis=1).reshape(-1, LAGS)
    stay_here = stays[0] == 1
    keep = jnp.where(stay_here, stay_part, move_part)
    got = across(jnp.where(stay_here, move_part, stay_part))
    low, high = jnp.where(core == 0, keep, got), jnp.where(core == 0, got, keep)
    others = channels * members
    as_stay = jnp.concatenate([low, high], axis=0).reshape(channels, others, LAGS)
    shape = (channels, members, 1, ROWS, LAGS)
    as_move = jnp.concatenate([low.reshape(shape), high.reshape(shape)], axis=2).reshape(channels, others, LAGS)
    return jnp.where(stay_here, as_stay, as_move)


def solution(mesh):
    placed = (P(("group", "member"), None, None), P())
    small = mesh.shape["group"] <= 8 and mesh.shape["member"] == 4
    return jax.shard_map(
        on_device_pairs if small else on_device_any,
        mesh=mesh,
        in_specs=placed,
        out_specs=P(("group", "member"), None, None),
        check_vma=False,
    )
```

```python
import itertools
import math

import jax
import jax.numpy as jnp
import ml_dtypes
import numpy as np
from jax import lax
from jax.experimental import pallas as pl
from jax.experimental.pallas import tpu as pltpu
from jax.sharding import PartitionSpec as P

LAGS = 128
HALF = 64
FINE = 16
ROWS = 16
VMEM_BYTES = 48 * 1024 * 1024


def lag_rows(freq_count, window_count):
    lag = np.arange(LAGS) - LAGS // 2
    freq = np.arange(freq_count)
    angle = np.pi * np.mod(lag[:, None] * freq[None, :], 2 * freq_count) / freq_count
    norm = 1.0 / math.sqrt(window_count * freq_count)
    rows = np.concatenate([np.cos(angle), -np.sin(angle)], axis=0) * norm
    return rows.astype(np.float32).astype(ml_dtypes.bfloat16)


def whiten_block(raw_ref, out_ref, wide_ref):
    rows, windows, width = raw_ref.shape
    freqs = width // 2
    lanes = windows * FINE
    groups = freqs // lanes
    for slab in range(2 * groups):
        value = raw_ref[:, :, slab * lanes : (slab + 1) * lanes].astype(jnp.float32)
        wide_ref[slab] = value.reshape(rows * windows, lanes)

    def window(slab, w):
        return wide_ref[slab, pl.ds(w, rows, stride=windows), :]

    pieces = []
    for group in range(groups):
        piece = jnp.zeros((rows, lanes), jnp.float32)
        for w in range(windows):
            real, imag = window(group, w), window(groups + group, w)
            piece += real * real + imag * imag
        pieces.append(piece)
    power = jnp.concatenate(pieces, axis=1)
    edge = jnp.zeros((rows, 2 * HALF), jnp.float32)
    padded = jnp.concatenate([edge, power, edge], axis=1)
    total = padded
    length = padded.shape[1]
    step = 1
    while step < 2 * HALF:
        total = total + pltpu.roll(total, length - step, axis=1)
        step *= 2
    total = total + pltpu.roll(padded, length - 2 * HALF, axis=1)
    smoothed = pltpu.roll(total, length - HALF, axis=1)[:, :freqs]
    place = lax.broadcasted_iota(jnp.int32, (rows, freqs), 1)
    counts = jnp.minimum(place + HALF, freqs - 1) - jnp.maximum(place - HALF, 0) + 1
    average = smoothed / (counts.astype(jnp.float32) * windows)
    factor = 1.0 / jnp.sqrt(average + 1e-05)
    granule = lax.broadcasted_iota(jnp.int32, (rows, lanes), 1) // FINE
    for part in range(2):
        for group in range(groups):
            scale = factor[:, group * lanes : (group + 1) * lanes]
            items = [window(part * groups + group, w) * scale for w in range(windows)]
            dist = windows // 2
            while dist:
                keep = (granule & dist) == 0
                nxt = list(items)
                for i in range(windows):
                    if i & dist:
                        continue
                    j = i + dist
                    nxt[i] = jnp.where(keep, items[i], pltpu.roll(items[j], dist * FINE, axis=1))
                    nxt[j] = jnp.where(keep, pltpu.roll(items[i], lanes - dist * FINE, axis=1), items[j])
                items = nxt
                dist //= 2
            for i in range(windows):
                out_ref[group * windows + i, :, part * lanes : (part + 1) * lanes] = items[i].astype(jnp.bfloat16)


def whiten(raw):
    channels, windows, width = raw.shape
    blocks = width // 2 // FINE
    return pl.pallas_call(
        whiten_block,
        grid=(channels // ROWS,),
        in_specs=[pl.BlockSpec((ROWS, windows, width), lambda i: (i, 0, 0))],
        out_specs=pl.BlockSpec((blocks, ROWS, 2 * windows * FINE), lambda i: (0, i, 0)),
        out_shape=jax.ShapeDtypeStruct((blocks, channels, 2 * windows * FINE), jnp.bfloat16),
        scratch_shapes=[pltpu.VMEM((blocks // windows * 2, ROWS * windows, windows * FINE), jnp.float32)],
        compiler_params=pltpu.CompilerParams(vmem_limit_bytes=VMEM_BYTES),
        name="whiten",
    )(raw)


def correlate_kernel(order_ref, a1, a2, b1, b2, b3, b4, table_ref, own_ref, other_ref, rows_ref, rhs_ref, cross_ref, flip_ref):
    step = pl.program_id(1)
    chunk, _, depth = a1.shape
    half = depth // 2
    a_count = 2 * ROWS
    b_count = 4 * ROWS
    width = 2 * b_count
    swap_a, swap_b, first_half = order_ref[0], order_ref[1], order_ref[2]
    fine_row = lax.broadcasted_iota(jnp.int32, (FINE, depth), 0)
    fine_lane = lax.broadcasted_iota(jnp.int32, (FINE, depth), 1) % FINE
    mask = (fine_row == fine_lane).astype(jnp.float32)

    for index, ref in enumerate((a1, a2)):
        at = pl.multiple_of((index ^ swap_a) * ROWS, ROWS)
        for f in range(chunk):
            rows_ref[f, pl.ds(at, ROWS), :] = ref[f].astype(jnp.float32)
    for index, ref in enumerate((b1, b2, b3, b4)):
        spot = ((index // 2) ^ swap_b) * 2 + ((index % 2) ^ first_half)
        at = pl.multiple_of(spot * ROWS, ROWS)
        for f in range(chunk):
            value = ref[f]
            rhs_ref[f, pl.ds(at, ROWS), :] = value
            rhs_ref[f, pl.ds(b_count + at, ROWS), :half] = -value[:, half:]
            rhs_ref[f, pl.ds(b_count + at, ROWS), half:] = value[:, :half]
    for f in range(chunk):
        parts = []
        for i in range(a_count):
            row = jnp.broadcast_to(rows_ref[f, i : i + 1, :], (FINE, depth))
            parts.append((row * mask).astype(jnp.bfloat16))
        left = jnp.concatenate(parts, axis=0)
        cross = lax.dot_general(
            left, rhs_ref[f], (((1,), (1,)), ((), ())), preferred_element_type=jnp.float32
        ).astype(jnp.bfloat16)
        at = pl.multiple_of((step * chunk + f) * FINE, FINE)
        for i in range(a_count):
            cross_ref[pl.ds(at, FINE), i * width : (i + 1) * width] = cross[i * FINE : (i + 1) * FINE]

    @pl.when(step == pl.num_programs(1) - 1)
    def _():
        low = lax.broadcasted_iota(jnp.int32, (LAGS, width), 1) < b_count
        for pair in range(a_count // 2):
            wide = jnp.dot(
                table_ref[...], cross_ref[:, 2 * pair * width : 2 * (pair + 1) * width], preferred_element_type=jnp.float32
            )
            for i in (2 * pair, 2 * pair + 1):
                both = wide[:, (i % 2) * width : (i % 2 + 1) * width]
                cos_part, sin_part = both[:LAGS], both[LAGS:]
                joined = jnp.where(
                    low,
                    cos_part + pltpu.roll(sin_part, b_count, axis=1),
                    pltpu.roll(cos_part, b_count, axis=1) - sin_part,
                )
                turned = joined.T
                own_ref[(i // ROWS) ^ swap_a, i % ROWS] = turned[:b_count].astype(jnp.bfloat16)
                flip_ref[pl.ds(i, b_count, stride=a_count), :] = turned[b_count:]
        span = b_count // 2 * a_count
        for index in range(2):
            value = flip_ref[index * span : (index + 1) * span, :].astype(jnp.bfloat16)
            other_ref[index ^ swap_b] = value.reshape(b_count // 2, a_count, LAGS)


def correlate(order, a_list, b_list, table, b_blocks, chunk=16):
    blocks, _, depth = a_list[0][0].shape
    freqs = blocks * FINE
    a_count, b_count = 2 * ROWS, 4 * ROWS
    width = 2 * b_count
    stride = 4 if b_blocks > 1 else 0

    def spec(offset, advance):
        return pl.BlockSpec((chunk, ROWS, depth), lambda j, s, *_: (s, offset + advance * j, 0))

    return pl.pallas_call(
        correlate_kernel,
        grid_spec=pltpu.PrefetchScalarGridSpec(
            num_scalar_prefetch=1,
            grid=(b_blocks, blocks // chunk),
            in_specs=[spec(o, 0) for _, o in a_list]
            + [spec(o, stride) for _, o in b_list]
            + [pl.BlockSpec((2 * LAGS, freqs), lambda j, s, *_: (0, 0))],
            out_specs=[
                pl.BlockSpec((2, ROWS, b_count, LAGS), lambda j, s, *_: (0, 0, j, 0)),
                pl.BlockSpec((2, b_count // 2, a_count, LAGS), lambda j, s, *_: (0, j, 0, 0)),
            ],
            scratch_shapes=[
                pltpu.VMEM((chunk, a_count, depth), jnp.float32),
                pltpu.VMEM((chunk, width, depth), jnp.bfloat16),
                pltpu.VMEM((freqs, a_count * width), jnp.bfloat16),
                pltpu.VMEM((b_count * a_count, LAGS), jnp.float32),
            ],
        ),
        out_shape=[
            jax.ShapeDtypeStruct((2, ROWS, b_blocks * b_count, LAGS), jnp.bfloat16),
            jax.ShapeDtypeStruct((2, b_blocks * b_count // 2, a_count, LAGS), jnp.bfloat16),
        ],
        compiler_params=pltpu.CompilerParams(
            vmem_limit_bytes=VMEM_BYTES, dimension_semantics=("arbitrary", "arbitrary")
        ),
        name="correlate",
    )(order, *[a for a, _ in a_list], *[b for b, _ in b_list], table)


def whiten_half(raw, which):
    channels, windows, width = raw.shape
    blocks = width // 2 // FINE
    depth = 2 * windows * FINE

    def kernel(which_ref, raw_ref, out_ref, wide_ref):
        whiten_block(raw_ref, out_ref, wide_ref)

    return pl.pallas_call(
        kernel,
        grid_spec=pltpu.PrefetchScalarGridSpec(
            num_scalar_prefetch=1,
            grid=(1,),
            in_specs=[pl.BlockSpec((ROWS, windows, width), lambda i, which_ref: (which_ref[0], 0, 0))],
            out_specs=pl.BlockSpec((blocks, ROWS, depth), lambda i, *_: (0, 0, 0)),
            scratch_shapes=[pltpu.VMEM((blocks // windows * 2, ROWS * windows, windows * FINE), jnp.float32)],
        ),
        out_shape=jax.ShapeDtypeStruct((blocks, ROWS, depth), jnp.bfloat16),
        compiler_params=pltpu.CompilerParams(vmem_limit_bytes=VMEM_BYTES),
        name="whiten_half",
    )(which, raw)


def whiten_sorted(raw, own, stays):
    rows, windows, width = raw.shape
    blocks, _, depth = own.shape

    def kernel(stays_ref, raw_ref, own_ref, stay_ref, move_ref, new_ref, wide_ref):
        whiten_block(raw_ref, new_ref, wide_ref)

        @pl.when(stays_ref[0] == 1)
        def _():
            stay_ref[...] = own_ref[...]
            move_ref[...] = new_ref[...]

        @pl.when(stays_ref[0] != 1)
        def _():
            stay_ref[...] = new_ref[...]
            move_ref[...] = own_ref[...]

    shape = jax.ShapeDtypeStruct(own.shape, jnp.bfloat16)
    return pl.pallas_call(
        kernel,
        in_specs=[
            pl.BlockSpec(memory_space=pltpu.SMEM),
            pl.BlockSpec(memory_space=pltpu.VMEM),
            pl.BlockSpec(memory_space=pltpu.VMEM),
        ],
        out_specs=[pl.BlockSpec(memory_space=pltpu.VMEM)] * 2,
        out_shape=[shape, shape],
        scratch_shapes=[
            pltpu.VMEM(own.shape, jnp.bfloat16),
            pltpu.VMEM((blocks // windows * 2, ROWS * windows, windows * FINE), jnp.float32),
        ],
        compiler_params=pltpu.CompilerParams(vmem_limit_bytes=VMEM_BYTES),
        name="whiten_sorted",
    )(stays, raw, own)


def assign_roles(partner):
    count = partner.shape[0]
    chips = count // 2

    def kernel(partner_ref, out_ref):
        for group in range(count):
            out_ref[group] = -1
        for group in range(count):

            @pl.when(out_ref[group] < 0)
            def _():
                def walk(_, here):
                    there = partner_ref[here]
                    out_ref[here] = 0
                    out_ref[there] = 1
                    return there ^ 1

                lax.fori_loop(0, chips, walk, jnp.int32(group))

        target = [partner_ref[2 * chip + 1 - out_ref[2 * chip]] // 2 for chip in range(chips)]
        rank = jnp.int32(0)
        for i in range(chips):
            for j in range(i + 1, chips):
                rank += jnp.where(target[j] < target[i], math.factorial(chips - 1 - i), 0)
        out_ref[count] = rank

    return pl.pallas_call(
        kernel,
        in_specs=[pl.BlockSpec(memory_space=pltpu.SMEM)],
        out_specs=pl.BlockSpec(memory_space=pltpu.SMEM),
        out_shape=jax.ShapeDtypeStruct((count + 1,), jnp.int32),
        name="assign_roles",
    )(partner)


def permute(value, groups, members, target):
    pairs = []
    for group, member in itertools.product(range(groups), range(members)):
        to_group, to_member = target(group, member)
        pairs.append((group * members + member, to_group * members + to_member))
    return lax.ppermute(value, ("group", "member"), pairs)


def on_device_any(spectra, partner):
    group_count = lax.axis_size("group")
    channels, windows, width = spectra.shape
    white = whiten(spectra)
    blocks, _, depth = white.shape
    spread = lax.all_to_all(white, "group", split_axis=1, concat_axis=1, tiled=True)
    shares = spread.reshape(blocks, group_count, channels // group_count, depth)
    ordered = jnp.take(shares, partner, axis=1).reshape(white.shape)
    arrived = lax.all_to_all(ordered, "group", split_axis=1, concat_axis=1, tiled=True)
    theirs = lax.all_gather(arrived, "member", axis=1, tiled=True)
    table = jnp.asarray(lag_rows(width // 2, windows))
    others = theirs.shape[1]
    order = jnp.zeros((3,), jnp.int32)
    result, _ = correlate(
        order, [(white, 0), (white, 1)], [(theirs, q) for q in range(4)], table, others // (4 * ROWS)
    )
    return result.reshape(channels, others, LAGS)


def on_device_pairs(spectra, partner):
    groups, members = lax.axis_size("group"), lax.axis_size("member")
    chips = groups // 2
    channels, windows, width = spectra.shape
    group, member = lax.axis_index("group"), lax.axis_index("member")
    core = group % 2

    def across(value):
        return permute(value, groups, members, lambda g, m: (g ^ 1, m))

    roles = assign_roles(partner)
    rank = roles[groups]
    stays = 1 - lax.dynamic_slice_in_dim(roles, group, 1)
    received = across(lax.dynamic_slice_in_dim(spectra, (1 - core) * ROWS, ROWS, 0))
    own = whiten_half(spectra, core.reshape(1))
    stay, move = whiten_sorted(received, own, stays)

    far = (2, 0, 3, 1)
    back = tuple(far.index(m) for m in range(members))
    near = (0, 2, 1, 3)
    orders = list(itertools.permutations(range(chips)))

    def go(order):
        def branch(stay, move):
            first = permute(stay, groups, members, lambda g, m: (g, far[m]))
            second = permute(stay, groups, members, lambda g, m: (g, near[m]))
            same = permute(move, groups, members, lambda g, m: (2 * order[g // 2] + g % 2, m))
            other = permute(move, groups, members, lambda g, m: (2 * order[g // 2] + g % 2, m ^ 1))
            return first, second, same, other

        return branch

    def home(order):
        def branch(first, second, same, other):
            first = permute(first, groups, members, lambda g, m: (g, back[m]))
            second = permute(second, groups, members, lambda g, m: (g, near[m]))
            same = permute(same, groups, members, lambda g, m: (2 * order.index(g // 2) + g % 2, m))
            other = permute(other, groups, members, lambda g, m: (2 * order.index(g // 2) + g % 2, m ^ 1))
            return first, second, same, other

        return branch

    first, second, here, there = lax.switch(rank, [go(order) for order in orders], stay, move)
    table = jnp.asarray(lag_rows(width // 2, windows))
    order = jnp.stack([(member < 2).astype(jnp.int32), member % 2, core])
    straight, mirrored = correlate(
        order,
        [(first, 0), (second, 0)],
        [(here, 0), (across(here), 0), (there, 0), (across(there), 0)],
        table,
        1,
    )
    from_far, from_near, here, there = lax.switch(
        rank, [home(order) for order in orders], straight[0], straight[1], mirrored[0], mirrored[1]
    )

    even = member % 2 == 0
    left, right = jnp.where(even, from_near, from_far), jnp.where(even, from_far, from_near)
    stay_part = jnp.concatenate([left, right], axis=1).reshape(-1, LAGS)
    left, right = jnp.where(even, here, there), jnp.where(even, there, here)
    move_part = jnp.concatenate([left, right], axis=1).reshape(-1, LAGS)
    stay_here = stays[0] == 1
    keep = jnp.where(stay_here, stay_part, move_part)
    got = across(jnp.where(stay_here, move_part, stay_part))
    low, high = jnp.where(core == 0, keep, got), jnp.where(core == 0, got, keep)
    others = channels * members
    as_stay = jnp.concatenate([low, high], axis=0).reshape(channels, others, LAGS)
    shape = (channels, members, 1, ROWS, LAGS)
    as_move = jnp.concatenate([low.reshape(shape), high.reshape(shape)], axis=2).reshape(channels, others, LAGS)
    return jnp.where(stay_here, as_stay, as_move)


def solution(mesh):
    placed = (P(("group", "member"), None, None), P())
    small = mesh.shape["group"] <= 8 and mesh.shape["member"] == 4
    return jax.shard_map(
        on_device_pairs if small else on_device_any,
        mesh=mesh,
        in_specs=placed,
        out_specs=P(("group", "member"), None, None),
        check_vma=False,
    )
```

```python
import itertools
import math

import jax
import jax.numpy as jnp
import ml_dtypes
import numpy as np
from jax import lax
from jax.experimental import pallas as pl
from jax.experimental.pallas import tpu as pltpu
from jax.sharding import PartitionSpec as P

LAGS = 128
HALF = 64
FINE = 16
ROWS = 16
VMEM_BYTES = 48 * 1024 * 1024


def lag_rows(freq_count, window_count):
    lag = np.arange(LAGS) - LAGS // 2
    freq = np.arange(freq_count)
    angle = np.pi * np.mod(lag[:, None] * freq[None, :], 2 * freq_count) / freq_count
    norm = 1.0 / math.sqrt(window_count * freq_count)
    rows = np.concatenate([np.cos(angle), -np.sin(angle)], axis=0) * norm
    return rows.astype(np.float32).astype(ml_dtypes.bfloat16)


def whiten_block(raw_ref, out_ref, wide_ref):
    rows, windows, width = raw_ref.shape
    freqs = width // 2
    lanes = windows * FINE
    groups = freqs // lanes
    for slab in range(2 * groups):
        value = raw_ref[:, :, slab * lanes : (slab + 1) * lanes].astype(jnp.float32)
        wide_ref[slab] = value.reshape(rows * windows, lanes)

    def window(slab, w):
        return wide_ref[slab, pl.ds(w, rows, stride=windows), :]

    pieces = []
    for group in range(groups):
        piece = jnp.zeros((rows, lanes), jnp.float32)
        for w in range(windows):
            real, imag = window(group, w), window(groups + group, w)
            piece += real * real + imag * imag
        pieces.append(piece)
    power = jnp.concatenate(pieces, axis=1)
    edge = jnp.zeros((rows, 2 * HALF), jnp.float32)
    padded = jnp.concatenate([edge, power, edge], axis=1)
    total = padded
    length = padded.shape[1]
    step = 1
    while step < 2 * HALF:
        total = total + pltpu.roll(total, length - step, axis=1)
        step *= 2
    total = total + pltpu.roll(padded, length - 2 * HALF, axis=1)
    smoothed = pltpu.roll(total, length - HALF, axis=1)[:, :freqs]
    place = lax.broadcasted_iota(jnp.int32, (rows, freqs), 1)
    counts = jnp.minimum(place + HALF, freqs - 1) - jnp.maximum(place - HALF, 0) + 1
    average = smoothed / (counts.astype(jnp.float32) * windows)
    factor = 1.0 / jnp.sqrt(average + 1e-05)
    granule = lax.broadcasted_iota(jnp.int32, (rows, lanes), 1) // FINE
    for part in range(2):
        for group in range(groups):
            scale = factor[:, group * lanes : (group + 1) * lanes]
            items = [window(part * groups + group, w) * scale for w in range(windows)]
            dist = windows // 2
            while dist:
                keep = (granule & dist) == 0
                nxt = list(items)
                for i in range(windows):
                    if i & dist:
                        continue
                    j = i + dist
                    nxt[i] = jnp.where(keep, items[i], pltpu.roll(items[j], dist * FINE, axis=1))
                    nxt[j] = jnp.where(keep, pltpu.roll(items[i], lanes - dist * FINE, axis=1), items[j])
                items = nxt
                dist //= 2
            for i in range(windows):
                out_ref[group * windows + i, :, part * lanes : (part + 1) * lanes] = items[i].astype(jnp.bfloat16)


def whiten(raw):
    channels, windows, width = raw.shape
    blocks = width // 2 // FINE
    return pl.pallas_call(
        whiten_block,
        grid=(channels // ROWS,),
        in_specs=[pl.BlockSpec((ROWS, windows, width), lambda i: (i, 0, 0))],
        out_specs=pl.BlockSpec((blocks, ROWS, 2 * windows * FINE), lambda i: (0, i, 0)),
        out_shape=jax.ShapeDtypeStruct((blocks, channels, 2 * windows * FINE), jnp.bfloat16),
        scratch_shapes=[pltpu.VMEM((blocks // windows * 2, ROWS * windows, windows * FINE), jnp.float32)],
        compiler_params=pltpu.CompilerParams(vmem_limit_bytes=VMEM_BYTES),
        name="whiten",
    )(raw)


def correlate_kernel(order_ref, a1, a2, b1, b2, b3, b4, table_ref, own_ref, other_ref, rows_ref, rhs_ref, cross_ref, flip_ref):
    step = pl.program_id(1)
    chunk, _, depth = a1.shape
    half = depth // 2
    a_count = 2 * ROWS
    b_count = 4 * ROWS
    width = 2 * b_count
    swap_a, swap_b, first_half = order_ref[0], order_ref[1], order_ref[2]
    fine_row = lax.broadcasted_iota(jnp.int32, (FINE, depth), 0)
    fine_lane = lax.broadcasted_iota(jnp.int32, (FINE, depth), 1) % FINE
    mask = (fine_row == fine_lane).astype(jnp.float32)

    for index, ref in enumerate((a1, a2)):
        at = pl.multiple_of((index ^ swap_a) * ROWS, ROWS)
        for f in range(chunk):
            rows_ref[f, pl.ds(at, ROWS), :] = ref[f].astype(jnp.float32)
    for index, ref in enumerate((b1, b2, b3, b4)):
        spot = ((index // 2) ^ swap_b) * 2 + ((index % 2) ^ first_half)
        at = pl.multiple_of(spot * ROWS, ROWS)
        for f in range(chunk):
            value = ref[f]
            rhs_ref[f, pl.ds(at, ROWS), :] = value
            rhs_ref[f, pl.ds(b_count + at, ROWS), :half] = -value[:, half:]
            rhs_ref[f, pl.ds(b_count + at, ROWS), half:] = value[:, :half]
    for f in range(chunk):
        parts = []
        for i in range(a_count):
            row = jnp.broadcast_to(rows_ref[f, i : i + 1, :], (FINE, depth))
            parts.append((row * mask).astype(jnp.bfloat16))
        left = jnp.concatenate(parts, axis=0)
        cross = lax.dot_general(
            left, rhs_ref[f], (((1,), (1,)), ((), ())), preferred_element_type=jnp.float32
        ).astype(jnp.bfloat16)
        at = pl.multiple_of((step * chunk + f) * FINE, FINE)
        for i in range(a_count):
            cross_ref[pl.ds(at, FINE), i * width : (i + 1) * width] = cross[i * FINE : (i + 1) * FINE]

    @pl.when(step == pl.num_programs(1) - 1)
    def _():
        low = lax.broadcasted_iota(jnp.int32, (LAGS, width), 1) < b_count
        for pair in range(a_count // 2):
            wide = jnp.dot(
                table_ref[...], cross_ref[:, 2 * pair * width : 2 * (pair + 1) * width], preferred_element_type=jnp.float32
            )
            for i in (2 * pair, 2 * pair + 1):
                both = wide[:, (i % 2) * width : (i % 2 + 1) * width]
                cos_part, sin_part = both[:LAGS], both[LAGS:]
                joined = jnp.where(
                    low,
                    cos_part + pltpu.roll(sin_part, b_count, axis=1),
                    pltpu.roll(cos_part, b_count, axis=1) - sin_part,
                )
                turned = joined.T
                own_ref[(i // ROWS) ^ swap_a, i % ROWS] = turned[:b_count].astype(jnp.bfloat16)
                flip_ref[pl.ds(i, b_count, stride=a_count), :] = turned[b_count:]
        span = b_count // 2 * a_count
        for index in range(2):
            value = flip_ref[index * span : (index + 1) * span, :].astype(jnp.bfloat16)
            other_ref[index ^ swap_b] = value.reshape(b_count // 2, a_count, LAGS)


def correlate(order, a_list, b_list, table, b_blocks, chunk=16):
    blocks, _, depth = a_list[0][0].shape
    freqs = blocks * FINE
    a_count, b_count = 2 * ROWS, 4 * ROWS
    width = 2 * b_count
    stride = 4 if b_blocks > 1 else 0

    def spec(offset, advance):
        return pl.BlockSpec((chunk, ROWS, depth), lambda j, s, *_: (s, offset + advance * j, 0))

    return pl.pallas_call(
        correlate_kernel,
        grid_spec=pltpu.PrefetchScalarGridSpec(
            num_scalar_prefetch=1,
            grid=(b_blocks, blocks // chunk),
            in_specs=[spec(o, 0) for _, o in a_list]
            + [spec(o, stride) for _, o in b_list]
            + [pl.BlockSpec((2 * LAGS, freqs), lambda j, s, *_: (0, 0))],
            out_specs=[
                pl.BlockSpec((2, ROWS, b_count, LAGS), lambda j, s, *_: (0, 0, j, 0)),
                pl.BlockSpec((2, b_count // 2, a_count, LAGS), lambda j, s, *_: (0, j, 0, 0)),
            ],
            scratch_shapes=[
                pltpu.VMEM((chunk, a_count, depth), jnp.float32),
                pltpu.VMEM((chunk, width, depth), jnp.bfloat16),
                pltpu.VMEM((freqs, a_count * width), jnp.bfloat16),
                pltpu.VMEM((b_count * a_count, LAGS), jnp.float32),
            ],
        ),
        out_shape=[
            jax.ShapeDtypeStruct((2, ROWS, b_blocks * b_count, LAGS), jnp.bfloat16),
            jax.ShapeDtypeStruct((2, b_blocks * b_count // 2, a_count, LAGS), jnp.bfloat16),
        ],
        compiler_params=pltpu.CompilerParams(
            vmem_limit_bytes=VMEM_BYTES, dimension_semantics=("arbitrary", "arbitrary")
        ),
        name="correlate",
    )(order, *[a for a, _ in a_list], *[b for b, _ in b_list], table)


def whiten_half(raw, info):
    channels, windows, width = raw.shape
    blocks = width // 2 // FINE
    depth = 2 * windows * FINE

    def kernel(info_ref, raw_ref, out_ref, wide_ref):
        whiten_block(raw_ref, out_ref, wide_ref)

    return pl.pallas_call(
        kernel,
        grid_spec=pltpu.PrefetchScalarGridSpec(
            num_scalar_prefetch=1,
            grid=(1,),
            in_specs=[pl.BlockSpec((ROWS, windows, width), lambda i, info_ref: (info_ref[2], 0, 0))],
            out_specs=pl.BlockSpec((blocks, ROWS, depth), lambda i, *_: (0, 0, 0)),
            scratch_shapes=[pltpu.VMEM((blocks // windows * 2, ROWS * windows, windows * FINE), jnp.float32)],
        ),
        out_shape=jax.ShapeDtypeStruct((blocks, ROWS, depth), jnp.bfloat16),
        compiler_params=pltpu.CompilerParams(vmem_limit_bytes=VMEM_BYTES),
        name="whiten_half",
    )(info, raw)


def whiten_sorted(raw, own, info):
    channels, windows, width = raw.shape
    blocks, _, depth = own.shape

    def kernel(info_ref, raw_ref, own_ref, stay_ref, move_ref, new_ref, wide_ref):
        whiten_block(raw_ref, new_ref, wide_ref)

        @pl.when(info_ref[3] == 1)
        def _():
            stay_ref[...] = own_ref[...]
            move_ref[...] = new_ref[...]

        @pl.when(info_ref[3] != 1)
        def _():
            stay_ref[...] = new_ref[...]
            move_ref[...] = own_ref[...]

    shape = jax.ShapeDtypeStruct(own.shape, jnp.bfloat16)
    whole = pl.BlockSpec((blocks, ROWS, depth), lambda i, *_: (0, 0, 0))
    return pl.pallas_call(
        kernel,
        grid_spec=pltpu.PrefetchScalarGridSpec(
            num_scalar_prefetch=1,
            grid=(1,),
            in_specs=[pl.BlockSpec((ROWS, windows, width), lambda i, info_ref: (info_ref[2], 0, 0)), whole],
            out_specs=[whole, whole],
            scratch_shapes=[
                pltpu.VMEM(own.shape, jnp.bfloat16),
                pltpu.VMEM((blocks // windows * 2, ROWS * windows, windows * FINE), jnp.float32),
            ],
        ),
        out_shape=[shape, shape],
        compiler_params=pltpu.CompilerParams(vmem_limit_bytes=VMEM_BYTES),
        name="whiten_sorted",
    )(info, raw, own)


def assign_roles(partner, members):
    count = partner.shape[0]
    chips = count // 2

    def kernel(partner_ref, rank_ref, info_ref, moves_ref):
        for group in range(count):
            moves_ref[group] = -1
        for group in range(count):

            @pl.when(moves_ref[group] < 0)
            def _():
                def walk(_, here):
                    there = partner_ref[here]
                    moves_ref[here] = 0
                    moves_ref[there] = 1
                    return there ^ 1

                lax.fori_loop(0, chips, walk, jnp.int32(group))

        target = [partner_ref[2 * chip + 1 - moves_ref[2 * chip]] // 2 for chip in range(chips)]
        rank = jnp.int32(0)
        for i in range(chips):
            for j in range(i + 1, chips):
                rank += jnp.where(target[j] < target[i], math.factorial(chips - 1 - i), 0)
        rank_ref[0] = rank
        group, member = lax.axis_index("group"), lax.axis_index("member")
        info_ref[0] = jnp.where(member < members // 2, 1, 0)
        info_ref[1] = member % 2
        info_ref[2] = group % 2
        info_ref[3] = 1 - moves_ref[group]

    return pl.pallas_call(
        kernel,
        in_specs=[pl.BlockSpec(memory_space=pltpu.SMEM)],
        out_specs=[pl.BlockSpec(memory_space=pltpu.SMEM)] * 2,
        out_shape=[jax.ShapeDtypeStruct((1,), jnp.int32), jax.ShapeDtypeStruct((4,), jnp.int32)],
        scratch_shapes=[pltpu.SMEM((count,), jnp.int32)],
        name="assign_roles",
    )(partner)


def assemble(info, pieces, got, members):
    far, near, here, there = pieces
    others = 2 * members * ROWS
    half = others // 2

    def kernel(info_ref, far_ref, near_ref, here_ref, there_ref, got_ref, out_ref):
        odd, core = info_ref[1], info_ref[2]

        def put_stay(side, low, value):
            at = pl.multiple_of(side * half, half)
            out_ref[pl.ds(low, ROWS), pl.ds(at, half), :] = value

        def put_move(side, which, value):
            for shard in range(2):
                at = pl.multiple_of(side * half + shard * 2 * ROWS + which * ROWS, ROWS)
                out_ref[:, pl.ds(at, ROWS), :] = value[:, shard * ROWS : (shard + 1) * ROWS, :]

        @pl.when(info_ref[3] == 1)
        def _():
            put_stay(1 - odd, core * ROWS, far_ref[...])
            put_stay(odd, core * ROWS, near_ref[...])
            put_stay(1 - odd, (1 - core) * ROWS, got_ref[0].reshape(far.shape))
            put_stay(odd, (1 - core) * ROWS, got_ref[1].reshape(near.shape))

        @pl.when(info_ref[3] != 1)
        def _():
            put_move(odd, core, here_ref[...])
            put_move(1 - odd, core, there_ref[...])
            put_move(odd, 1 - core, got_ref[0].reshape(here.shape))
            put_move(1 - odd, 1 - core, got_ref[1].reshape(there.shape))

    return pl.pallas_call(
        kernel,
        in_specs=[pl.BlockSpec(memory_space=pltpu.SMEM)] + [pl.BlockSpec(memory_space=pltpu.VMEM)] * 5,
        out_specs=pl.BlockSpec(memory_space=pltpu.VMEM),
        out_shape=jax.ShapeDtypeStruct((2 * ROWS, others, LAGS), jnp.bfloat16),
        compiler_params=pltpu.CompilerParams(vmem_limit_bytes=VMEM_BYTES),
        name="assemble",
    )(info, far, near, here, there, got)


def permute(value, groups, members, target):
    pairs = []
    for group, member in itertools.product(range(groups), range(members)):
        to_group, to_member = target(group, member)
        pairs.append((group * members + member, to_group * members + to_member))
    return lax.ppermute(value, ("group", "member"), pairs)


def on_device_any(spectra, partner):
    group_count = lax.axis_size("group")
    channels, windows, width = spectra.shape
    white = whiten(spectra)
    blocks, _, depth = white.shape
    spread = lax.all_to_all(white, "group", split_axis=1, concat_axis=1, tiled=True)
    shares = spread.reshape(blocks, group_count, channels // group_count, depth)
    ordered = jnp.take(shares, partner, axis=1).reshape(white.shape)
    arrived = lax.all_to_all(ordered, "group", split_axis=1, concat_axis=1, tiled=True)
    theirs = lax.all_gather(arrived, "member", axis=1, tiled=True)
    table = jnp.asarray(lag_rows(width // 2, windows))
    others = theirs.shape[1]
    order = jnp.zeros((3,), jnp.int32)
    result, _ = correlate(
        order, [(white, 0), (white, 1)], [(theirs, q) for q in range(4)], table, others // (4 * ROWS)
    )
    return result.reshape(channels, others, LAGS)


def on_device_pairs(spectra, partner):
    groups, members = lax.axis_size("group"), lax.axis_size("member")
    chips = groups // 2
    windows, width = spectra.shape[1:]

    def across(value):
        return permute(value, groups, members, lambda g, m: (g ^ 1, m))

    rank, info = assign_roles(partner, members)
    own = whiten_half(spectra, info)
    stay, move = whiten_sorted(across(spectra), own, info)

    far = (2, 0, 3, 1)
    back = tuple(far.index(m) for m in range(members))
    near = (0, 2, 1, 3)
    orders = list(itertools.permutations(range(chips)))

    def go(order):
        def branch(stay, move):
            first = permute(stay, groups, members, lambda g, m: (g, far[m]))
            second = permute(stay, groups, members, lambda g, m: (g, near[m]))
            same = permute(move, groups, members, lambda g, m: (2 * order[g // 2] + g % 2, m))
            other = permute(move, groups, members, lambda g, m: (2 * order[g // 2] + g % 2, m ^ 1))
            return first, second, same, across(same), other, across(other)

        return branch

    def home(order):
        def branch(first, second, same, other):
            first = permute(first, groups, members, lambda g, m: (g, back[m]))
            second = permute(second, groups, members, lambda g, m: (g, near[m]))
            same = permute(same, groups, members, lambda g, m: (2 * order.index(g // 2) + g % 2, m))
            other = permute(other, groups, members, lambda g, m: (2 * order.index(g // 2) + g % 2, m ^ 1))
            return first, second, same, other

        return branch

    first, second, here, here_too, there, there_too = lax.switch(
        rank[0], [go(order) for order in orders], stay, move
    )
    table = jnp.asarray(lag_rows(width // 2, windows))
    straight, mirrored = correlate(
        info,
        [(first, 0), (second, 0)],
        [(here, 0), (here_too, 0), (there, 0), (there_too, 0)],
        table,
        1,
    )
    pieces = lax.switch(
        rank[0], [home(order) for order in orders], straight[0], straight[1], mirrored[0], mirrored[1]
    )
    flat = [piece.reshape(-1, LAGS) for piece in pieces]
    sent = jnp.where(info[3] == 1, jnp.stack(flat[2:]), jnp.stack(flat[:2]))
    return assemble(info, pieces, across(sent), members)


def solution(mesh):
    placed = (P(("group", "member"), None, None), P())
    small = mesh.shape["group"] <= 8 and mesh.shape["member"] == 4
    return jax.shard_map(
        on_device_pairs if small else on_device_any,
        mesh=mesh,
        in_specs=placed,
        out_specs=P(("group", "member"), None, None),
        check_vma=False,
    )
```

```python
import itertools
import math

import jax
import jax.numpy as jnp
import ml_dtypes
import numpy as np
from jax import lax
from jax.experimental import pallas as pl
from jax.experimental.pallas import tpu as pltpu
from jax.sharding import PartitionSpec as P

LAGS = 128
HALF = 64
FINE = 16
ROWS = 16
VMEM_BYTES = 48 * 1024 * 1024


def lag_rows(freq_count, window_count):
    lag = np.arange(LAGS) - LAGS // 2
    freq = np.arange(freq_count)
    angle = np.pi * np.mod(lag[:, None] * freq[None, :], 2 * freq_count) / freq_count
    norm = 1.0 / math.sqrt(window_count * freq_count)
    rows = np.concatenate([np.cos(angle), -np.sin(angle)], axis=0) * norm
    return rows.astype(np.float32).astype(ml_dtypes.bfloat16)


def whiten_block(raw_ref, out_ref, wide_ref):
    rows, windows, width = raw_ref.shape
    freqs = width // 2
    lanes = windows * FINE
    groups = freqs // lanes
    for slab in range(2 * groups):
        value = raw_ref[:, :, slab * lanes : (slab + 1) * lanes].astype(jnp.float32)
        wide_ref[slab] = value.reshape(rows * windows, lanes)

    def window(slab, w):
        return wide_ref[slab, pl.ds(w, rows, stride=windows), :]

    pieces = []
    for group in range(groups):
        piece = jnp.zeros((rows, lanes), jnp.float32)
        for w in range(windows):
            real, imag = window(group, w), window(groups + group, w)
            piece += real * real + imag * imag
        pieces.append(piece)
    power = jnp.concatenate(pieces, axis=1)
    edge = jnp.zeros((rows, 2 * HALF), jnp.float32)
    padded = jnp.concatenate([edge, power, edge], axis=1)
    total = padded
    length = padded.shape[1]
    step = 1
    while step < 2 * HALF:
        total = total + pltpu.roll(total, length - step, axis=1)
        step *= 2
    total = total + pltpu.roll(padded, length - 2 * HALF, axis=1)
    smoothed = pltpu.roll(total, length - HALF, axis=1)[:, :freqs]
    place = lax.broadcasted_iota(jnp.int32, (rows, freqs), 1)
    counts = jnp.minimum(place + HALF, freqs - 1) - jnp.maximum(place - HALF, 0) + 1
    average = smoothed / (counts.astype(jnp.float32) * windows)
    factor = 1.0 / jnp.sqrt(average + 1e-05)
    granule = lax.broadcasted_iota(jnp.int32, (rows, lanes), 1) // FINE
    for part in range(2):
        for group in range(groups):
            scale = factor[:, group * lanes : (group + 1) * lanes]
            items = [window(part * groups + group, w) * scale for w in range(windows)]
            dist = windows // 2
            while dist:
                keep = (granule & dist) == 0
                nxt = list(items)
                for i in range(windows):
                    if i & dist:
                        continue
                    j = i + dist
                    nxt[i] = jnp.where(keep, items[i], pltpu.roll(items[j], dist * FINE, axis=1))
                    nxt[j] = jnp.where(keep, pltpu.roll(items[i], lanes - dist * FINE, axis=1), items[j])
                items = nxt
                dist //= 2
            for i in range(windows):
                out_ref[group * windows + i, :, part * lanes : (part + 1) * lanes] = items[i].astype(jnp.bfloat16)


def whiten(raw):
    channels, windows, width = raw.shape
    blocks = width // 2 // FINE
    return pl.pallas_call(
        whiten_block,
        grid=(channels // ROWS,),
        in_specs=[pl.BlockSpec((ROWS, windows, width), lambda i: (i, 0, 0))],
        out_specs=pl.BlockSpec((blocks, ROWS, 2 * windows * FINE), lambda i: (0, i, 0)),
        out_shape=jax.ShapeDtypeStruct((blocks, channels, 2 * windows * FINE), jnp.bfloat16),
        scratch_shapes=[pltpu.VMEM((blocks // windows * 2, ROWS * windows, windows * FINE), jnp.float32)],
        compiler_params=pltpu.CompilerParams(vmem_limit_bytes=VMEM_BYTES),
        name="whiten",
    )(raw)


def correlate_kernel(order_ref, a1, a2, b1, b2, b3, b4, table_ref, own_ref, other_ref, rows_ref, rhs_ref, cross_ref, flip_ref):
    step = pl.program_id(1)
    chunk, _, depth = a1.shape
    half = depth // 2
    a_count = 2 * ROWS
    b_count = 4 * ROWS
    width = 2 * b_count
    swap_a, swap_b, first_half = order_ref[0], order_ref[1], order_ref[2]
    part = FINE // 2
    lane = lax.broadcasted_iota(jnp.int32, (part, depth), 1)
    mask = (lane % part == lax.broadcasted_iota(jnp.int32, (part, depth), 0)).astype(jnp.float32)
    upper = (lax.broadcasted_iota(jnp.int32, (ROWS, depth), 1) // part % 2).astype(jnp.float32)
    upper = upper.astype(jnp.bfloat16)
    sides = (1 - upper, upper)

    for index, ref in enumerate((a1, a2)):
        at = pl.multiple_of((index ^ swap_a) * ROWS, ROWS)
        for f in range(chunk):
            rows_ref[f, pl.ds(at, ROWS), :] = ref[f].astype(jnp.float32)
    for index, ref in enumerate((b1, b2, b3, b4)):
        spot = ((index // 2) ^ swap_b) * 2 + ((index % 2) ^ first_half)
        at = pl.multiple_of(spot * ROWS, ROWS)
        for f in range(chunk):
            value = ref[f]
            turned = jnp.concatenate([-value[:, half:], value[:, :half]], axis=1)
            for side in range(2):
                rhs_ref[f, pl.ds(side * width + at, ROWS), :] = value * sides[side]
                rhs_ref[f, pl.ds(side * width + b_count + at, ROWS), :] = turned * sides[side]
    for f in range(chunk):
        parts = []
        for i in range(a_count):
            parts.append(jnp.broadcast_to(rows_ref[f, i : i + 1, :], (part, depth)) * mask)
        left = jnp.concatenate(parts, axis=0).astype(jnp.bfloat16)
        cross = lax.dot_general(
            left, rhs_ref[f], (((1,), (1,)), ((), ())), preferred_element_type=jnp.float32
        )
        at = pl.multiple_of((step * chunk + f) * FINE, FINE)
        for i in range(a_count):
            rows = cross[i * part : (i + 1) * part]
            both = jnp.concatenate([rows[:, :width], rows[:, width:]], axis=0)
            cross_ref[pl.ds(at, FINE), i * width : (i + 1) * width] = both.astype(jnp.bfloat16)

    @pl.when(step == pl.num_programs(1) - 1)
    def _():
        low = lax.broadcasted_iota(jnp.int32, (LAGS, width), 1) < b_count
        for pair in range(a_count // 2):
            wide = jnp.dot(
                table_ref[...], cross_ref[:, 2 * pair * width : 2 * (pair + 1) * width], preferred_element_type=jnp.float32
            )
            for i in (2 * pair, 2 * pair + 1):
                both = wide[:, (i % 2) * width : (i % 2 + 1) * width]
                cos_part, sin_part = both[:LAGS], both[LAGS:]
                joined = jnp.where(
                    low,
                    cos_part + pltpu.roll(sin_part, b_count, axis=1),
                    pltpu.roll(cos_part, b_count, axis=1) - sin_part,
                )
                turned = joined.T
                at = i % ROWS * b_count
                own_ref[(i // ROWS) ^ swap_a, at : at + b_count, :] = turned[:b_count].astype(jnp.bfloat16)
                flip_ref[pl.ds(i, b_count, stride=a_count), :] = turned[b_count:]
        span = b_count // 2 * a_count
        for index in range(2):
            value = flip_ref[index * span : (index + 1) * span, :].astype(jnp.bfloat16)
            other_ref[index ^ swap_b] = value


def correlate(order, a_list, b_list, table, b_blocks, chunk=16):
    blocks, _, depth = a_list[0][0].shape
    freqs = blocks * FINE
    a_count, b_count = 2 * ROWS, 4 * ROWS
    width = 2 * b_count
    stride = 4 if b_blocks > 1 else 0

    def spec(offset, advance):
        return pl.BlockSpec((chunk, ROWS, depth), lambda j, s, *_: (s, offset + advance * j, 0))

    return pl.pallas_call(
        correlate_kernel,
        grid_spec=pltpu.PrefetchScalarGridSpec(
            num_scalar_prefetch=1,
            grid=(b_blocks, blocks // chunk),
            in_specs=[spec(o, 0) for _, o in a_list]
            + [spec(o, stride) for _, o in b_list]
            + [pl.BlockSpec((2 * LAGS, freqs), lambda j, s, *_: (0, 0))],
            out_specs=[
                pl.BlockSpec((2, ROWS * b_count, LAGS), lambda j, s, *_: (0, j, 0)),
                pl.BlockSpec((2, b_count // 2 * a_count, LAGS), lambda j, s, *_: (0, j, 0)),
            ],
            scratch_shapes=[
                pltpu.VMEM((chunk, a_count, depth), jnp.float32),
                pltpu.VMEM((chunk, 2 * width, depth), jnp.bfloat16),
                pltpu.VMEM((freqs, a_count * width), jnp.bfloat16),
                pltpu.VMEM((b_count * a_count, LAGS), jnp.float32),
            ],
        ),
        out_shape=[
            jax.ShapeDtypeStruct((2, b_blocks * ROWS * b_count, LAGS), jnp.bfloat16),
            jax.ShapeDtypeStruct((2, b_blocks * b_count // 2 * a_count, LAGS), jnp.bfloat16),
        ],
        compiler_params=pltpu.CompilerParams(
            vmem_limit_bytes=VMEM_BYTES, dimension_semantics=("arbitrary", "arbitrary")
        ),
        name="correlate",
    )(order, *[a for a, _ in a_list], *[b for b, _ in b_list], table)


def whiten_half(raw, info):
    channels, windows, width = raw.shape
    blocks = width // 2 // FINE
    depth = 2 * windows * FINE

    def kernel(info_ref, raw_ref, out_ref, half_ref, wide_ref, sem):
        low = pl.multiple_of(info_ref[2] * ROWS, ROWS)
        copy = pltpu.make_async_copy(raw_ref.at[pl.ds(low, ROWS)], half_ref, sem)
        copy.start()
        copy.wait()
        whiten_block(half_ref, out_ref, wide_ref)

    return pl.pallas_call(
        kernel,
        in_specs=[pl.BlockSpec(memory_space=pltpu.SMEM), pl.BlockSpec(memory_space=pltpu.HBM)],
        out_specs=pl.BlockSpec(memory_space=pltpu.VMEM),
        out_shape=jax.ShapeDtypeStruct((blocks, ROWS, depth), jnp.bfloat16),
        scratch_shapes=[
            pltpu.VMEM((ROWS, windows, width), jnp.bfloat16),
            pltpu.VMEM((blocks // windows * 2, ROWS * windows, windows * FINE), jnp.float32),
            pltpu.SemaphoreType.DMA(()),
        ],
        compiler_params=pltpu.CompilerParams(vmem_limit_bytes=VMEM_BYTES),
        name="whiten_half",
    )(info, raw)


def whiten_sorted(raw, own, info):
    channels, windows, width = raw.shape
    blocks, _, depth = own.shape

    def kernel(info_ref, raw_ref, own_ref, stay_ref, move_ref, new_ref, wide_ref):
        whiten_block(raw_ref, new_ref, wide_ref)

        @pl.when(info_ref[3] == 1)
        def _():
            stay_ref[...] = own_ref[...]
            move_ref[...] = new_ref[...]

        @pl.when(info_ref[3] != 1)
        def _():
            stay_ref[...] = new_ref[...]
            move_ref[...] = own_ref[...]

    shape = jax.ShapeDtypeStruct(own.shape, jnp.bfloat16)
    whole = pl.BlockSpec((blocks, ROWS, depth), lambda i, *_: (0, 0, 0))
    return pl.pallas_call(
        kernel,
        grid_spec=pltpu.PrefetchScalarGridSpec(
            num_scalar_prefetch=1,
            grid=(1,),
            in_specs=[pl.BlockSpec((ROWS, windows, width), lambda i, info_ref: (info_ref[2], 0, 0)), whole],
            out_specs=[whole, whole],
            scratch_shapes=[
                pltpu.VMEM(own.shape, jnp.bfloat16),
                pltpu.VMEM((blocks // windows * 2, ROWS * windows, windows * FINE), jnp.float32),
            ],
        ),
        out_shape=[shape, shape],
        compiler_params=pltpu.CompilerParams(vmem_limit_bytes=VMEM_BYTES),
        name="whiten_sorted",
    )(info, raw, own)


def assign_roles(partner, members):
    count = partner.shape[0]
    chips = count // 2

    def kernel(partner_ref, rank_ref, info_ref, moves_ref):
        for group in range(count):
            moves_ref[group] = -1
        for group in range(count):

            @pl.when(moves_ref[group] < 0)
            def _():
                def walk(_, here):
                    there = partner_ref[here]
                    moves_ref[here] = 0
                    moves_ref[there] = 1
                    return there ^ 1

                lax.fori_loop(0, chips, walk, jnp.int32(group))

        target = [partner_ref[2 * chip + 1 - moves_ref[2 * chip]] // 2 for chip in range(chips)]
        rank = jnp.int32(0)
        for i in range(chips):
            for j in range(i + 1, chips):
                rank += jnp.where(target[j] < target[i], math.factorial(chips - 1 - i), 0)
        rank_ref[0] = rank
        group, member = lax.axis_index("group"), lax.axis_index("member")
        info_ref[0] = jnp.where(member < members // 2, 1, 0)
        info_ref[1] = member % 2
        info_ref[2] = group % 2
        info_ref[3] = 1 - moves_ref[group]

    return pl.pallas_call(
        kernel,
        in_specs=[pl.BlockSpec(memory_space=pltpu.SMEM)],
        out_specs=[pl.BlockSpec(memory_space=pltpu.SMEM)] * 2,
        out_shape=[jax.ShapeDtypeStruct((1,), jnp.int32), jax.ShapeDtypeStruct((4,), jnp.int32)],
        scratch_shapes=[pltpu.SMEM((count,), jnp.int32)],
        name="assign_roles",
    )(partner)


def assemble(info, pieces, got, members):
    others = 2 * members * ROWS
    half = others // 2

    def kernel(info_ref, far_ref, near_ref, here_ref, there_ref, got_ref, out_ref):
        odd, core = info_ref[1], info_ref[2]

        def put_stay(side, which, ref):
            low = pl.multiple_of(which * ROWS, ROWS)
            at = pl.multiple_of(side * half, half)
            out_ref[pl.ds(low, ROWS), pl.ds(at, half), :] = ref[...].reshape(ROWS, half, LAGS)

        def put_move(side, which, ref):
            value = ref[...].reshape(2 * ROWS, 2 * ROWS, LAGS)
            for shard in range(2):
                at = pl.multiple_of(side * half + shard * 2 * ROWS + which * ROWS, ROWS)
                out_ref[:, pl.ds(at, ROWS), :] = value[:, shard * ROWS : (shard + 1) * ROWS, :]

        @pl.when(info_ref[3] == 1)
        def _():
            put_stay(1 - odd, core, far_ref)
            put_stay(odd, core, near_ref)
            put_stay(1 - odd, 1 - core, got_ref.at[0])
            put_stay(odd, 1 - core, got_ref.at[1])

        @pl.when(info_ref[3] != 1)
        def _():
            put_move(odd, core, here_ref)
            put_move(1 - odd, core, there_ref)
            put_move(odd, 1 - core, got_ref.at[0])
            put_move(1 - odd, 1 - core, got_ref.at[1])

    return pl.pallas_call(
        kernel,
        in_specs=[pl.BlockSpec(memory_space=pltpu.SMEM)] + [pl.BlockSpec(memory_space=pltpu.VMEM)] * 5,
        out_specs=pl.BlockSpec(memory_space=pltpu.VMEM),
        out_shape=jax.ShapeDtypeStruct((2 * ROWS, others, LAGS), jnp.bfloat16),
        compiler_params=pltpu.CompilerParams(vmem_limit_bytes=VMEM_BYTES),
        name="assemble",
    )(info, *pieces, got)


def permute(value, groups, members, target):
    pairs = []
    for group, member in itertools.product(range(groups), range(members)):
        to_group, to_member = target(group, member)
        pairs.append((group * members + member, to_group * members + to_member))
    return lax.ppermute(value, ("group", "member"), pairs)


def on_device_any(spectra, partner):
    group_count = lax.axis_size("group")
    channels, windows, width = spectra.shape
    white = whiten(spectra)
    blocks, _, depth = white.shape
    spread = lax.all_to_all(white, "group", split_axis=1, concat_axis=1, tiled=True)
    shares = spread.reshape(blocks, group_count, channels // group_count, depth)
    ordered = jnp.take(shares, partner, axis=1).reshape(white.shape)
    arrived = lax.all_to_all(ordered, "group", split_axis=1, concat_axis=1, tiled=True)
    theirs = lax.all_gather(arrived, "member", axis=1, tiled=True)
    table = jnp.asarray(lag_rows(width // 2, windows))
    others = theirs.shape[1]
    order = jnp.zeros((3,), jnp.int32)
    result, _ = correlate(
        order, [(white, 0), (white, 1)], [(theirs, q) for q in range(4)], table, others // (4 * ROWS)
    )
    result = result.reshape(2, others // (4 * ROWS), ROWS, 4 * ROWS, LAGS)
    return jnp.transpose(result, (0, 2, 1, 3, 4)).reshape(channels, others, LAGS)


def on_device_pairs(spectra, partner):
    groups, members = lax.axis_size("group"), lax.axis_size("member")
    chips = groups // 2
    windows, width = spectra.shape[1:]

    def across(value):
        return permute(value, groups, members, lambda g, m: (g ^ 1, m))

    rank, info = assign_roles(partner, members)
    own = whiten_half(spectra, info)
    stay, move = whiten_sorted(across(spectra), own, info)

    far = (2, 0, 3, 1)
    back = tuple(far.index(m) for m in range(members))
    near = (0, 2, 1, 3)
    orders = list(itertools.permutations(range(chips)))

    def straight_way(order):
        return sum(order[chip] == chips - 1 - chip for chip in range(chips)) < 2

    def go(order):
        def branch(stay, move):
            def go_on(value, flip):
                return permute(value, groups, members, lambda g, m: (2 * order[g // 2] + g % 2, m ^ flip))

            here = go_on(move, 0)
            first = permute(stay, groups, members, lambda g, m: (g, far[m]))
            if straight_way(order):
                there = go_on(move, 1)
            else:
                barred, _, stay = lax.optimization_barrier((here, first, stay))
                there = permute(barred, groups, members, lambda g, m: (g, m ^ 1))
            second = permute(stay, groups, members, lambda g, m: (g, near[m]))
            return first, second, here, across(here), there, across(there)

        return branch

    def home(order):
        def branch(first, second, same, other):
            def back_home(value, flip):
                return permute(value, groups, members, lambda g, m: (2 * order.index(g // 2) + g % 2, m ^ flip))

            here = back_home(same, 0)
            from_near = permute(second, groups, members, lambda g, m: (g, near[m]))
            if straight_way(order):
                there = back_home(other, 1)
            else:
                swapped = permute(other, groups, members, lambda g, m: (g, m ^ 1))
                first, swapped, _, _ = lax.optimization_barrier((first, swapped, from_near, here))
                there = back_home(swapped, 0)
            from_far = permute(first, groups, members, lambda g, m: (g, back[m]))
            return from_far, from_near, here, there

        return branch

    first, second, here, here_too, there, there_too = lax.switch(
        rank[0], [go(order) for order in orders], stay, move
    )
    table = jnp.asarray(lag_rows(width // 2, windows))
    straight, mirrored = correlate(
        info,
        [(first, 0), (second, 0)],
        [(here, 0), (here_too, 0), (there, 0), (there_too, 0)],
        table,
        1,
    )
    pieces = lax.switch(
        rank[0], [home(order) for order in orders], straight[0], straight[1], mirrored[0], mirrored[1]
    )
    far_piece, near_piece, here_piece, there_piece = pieces
    sent = jnp.where(info[3] == 1, jnp.stack([here_piece, there_piece]), jnp.stack([far_piece, near_piece]))
    return assemble(info, pieces, across(sent), members)


def solution(mesh):
    placed = (P(("group", "member"), None, None), P())
    small = mesh.shape["group"] <= 8 and mesh.shape["member"] == 4
    return jax.shard_map(
        on_device_pairs if small else on_device_any,
        mesh=mesh,
        in_specs=placed,
        out_specs=P(("group", "member"), None, None),
        check_vma=False,
    )
```

```python
import itertools
import math

import jax
import jax.numpy as jnp
import ml_dtypes
import numpy as np
from jax import lax
from jax.experimental import pallas as pl
from jax.experimental.pallas import tpu as pltpu
from jax.sharding import PartitionSpec as P

LAGS = 128
HALF = 64
FINE = 16
ROWS = 16
VMEM_BYTES = 48 * 1024 * 1024


def lag_rows(freq_count, window_count):
    lag = np.arange(LAGS) - LAGS // 2
    freq = np.arange(freq_count)
    angle = np.pi * np.mod(lag[:, None] * freq[None, :], 2 * freq_count) / freq_count
    norm = 1.0 / math.sqrt(window_count * freq_count)
    rows = np.concatenate([np.cos(angle), -np.sin(angle)], axis=0) * norm
    return rows.astype(np.float32).astype(ml_dtypes.bfloat16)


def whiten_block(raw_ref, out_ref, wide_ref):
    rows, windows, width = raw_ref.shape
    freqs = width // 2
    lanes = windows * FINE
    groups = freqs // lanes
    for slab in range(2 * groups):
        value = raw_ref[:, :, slab * lanes : (slab + 1) * lanes].astype(jnp.float32)
        wide_ref[slab] = value.reshape(rows * windows, lanes)

    def window(slab, w):
        return wide_ref[slab, pl.ds(w, rows, stride=windows), :]

    pieces = []
    for group in range(groups):
        piece = jnp.zeros((rows, lanes), jnp.float32)
        for w in range(windows):
            real, imag = window(group, w), window(groups + group, w)
            piece += real * real + imag * imag
        pieces.append(piece)
    power = jnp.concatenate(pieces, axis=1)
    edge = jnp.zeros((rows, 2 * HALF), jnp.float32)
    padded = jnp.concatenate([edge, power, edge], axis=1)
    total = padded
    length = padded.shape[1]
    step = 1
    while step < 2 * HALF:
        total = total + pltpu.roll(total, length - step, axis=1)
        step *= 2
    total = total + pltpu.roll(padded, length - 2 * HALF, axis=1)
    smoothed = pltpu.roll(total, length - HALF, axis=1)[:, :freqs]
    place = lax.broadcasted_iota(jnp.int32, (rows, freqs), 1)
    counts = jnp.minimum(place + HALF, freqs - 1) - jnp.maximum(place - HALF, 0) + 1
    average = smoothed / (counts.astype(jnp.float32) * windows)
    factor = 1.0 / jnp.sqrt(average + 1e-05)
    granule = lax.broadcasted_iota(jnp.int32, (rows, lanes), 1) // FINE
    for part in range(2):
        for group in range(groups):
            scale = factor[:, group * lanes : (group + 1) * lanes]
            items = [window(part * groups + group, w) * scale for w in range(windows)]
            dist = windows // 2
            while dist:
                keep = (granule & dist) == 0
                nxt = list(items)
                for i in range(windows):
                    if i & dist:
                        continue
                    j = i + dist
                    nxt[i] = jnp.where(keep, items[i], pltpu.roll(items[j], dist * FINE, axis=1))
                    nxt[j] = jnp.where(keep, pltpu.roll(items[i], lanes - dist * FINE, axis=1), items[j])
                items = nxt
                dist //= 2
            for i in range(windows):
                out_ref[group * windows + i, :, part * lanes : (part + 1) * lanes] = items[i].astype(jnp.bfloat16)


def whiten(raw):
    channels, windows, width = raw.shape
    blocks = width // 2 // FINE
    return pl.pallas_call(
        whiten_block,
        grid=(channels // ROWS,),
        in_specs=[pl.BlockSpec((ROWS, windows, width), lambda i: (i, 0, 0))],
        out_specs=pl.BlockSpec((blocks, ROWS, 2 * windows * FINE), lambda i: (0, i, 0)),
        out_shape=jax.ShapeDtypeStruct((blocks, channels, 2 * windows * FINE), jnp.bfloat16),
        scratch_shapes=[pltpu.VMEM((blocks // windows * 2, ROWS * windows, windows * FINE), jnp.float32)],
        compiler_params=pltpu.CompilerParams(vmem_limit_bytes=VMEM_BYTES),
        name="whiten",
    )(raw)


def correlate_kernel(order_ref, a1, a2, b1, b2, b3, b4, table_ref, own_ref, other_ref, rows_ref, rhs_ref, cross_ref, flip_ref):
    step = pl.program_id(1)
    chunk, _, depth = a1.shape
    half = depth // 2
    a_count = 2 * ROWS
    b_count = 4 * ROWS
    width = 2 * b_count
    swap_a, swap_b, first_half = order_ref[0], order_ref[1], order_ref[2]
    part = FINE // 2
    lane = lax.broadcasted_iota(jnp.int32, (part, depth), 1)
    mask = (lane % part == lax.broadcasted_iota(jnp.int32, (part, depth), 0)).astype(jnp.float32)
    upper = (lax.broadcasted_iota(jnp.int32, (ROWS, depth), 1) // part % 2).astype(jnp.float32)
    upper = upper.astype(jnp.bfloat16)
    sides = (1 - upper, upper)

    for index, ref in enumerate((a1, a2)):
        at = pl.multiple_of((index ^ swap_a) * ROWS, ROWS)
        for f in range(chunk):
            rows_ref[f, pl.ds(at, ROWS), :] = ref[f].astype(jnp.float32)
    for index, ref in enumerate((b1, b2, b3, b4)):
        spot = ((index // 2) ^ swap_b) * 2 + ((index % 2) ^ first_half)
        at = pl.multiple_of(spot * ROWS, ROWS)
        for f in range(chunk):
            value = ref[f]
            turned = jnp.concatenate([-value[:, half:], value[:, :half]], axis=1)
            for side in range(2):
                rhs_ref[f, pl.ds(side * width + at, ROWS), :] = value * sides[side]
                rhs_ref[f, pl.ds(side * width + b_count + at, ROWS), :] = turned * sides[side]
    for f in range(chunk):
        parts = []
        for i in range(a_count):
            parts.append(jnp.broadcast_to(rows_ref[f, i : i + 1, :], (part, depth)) * mask)
        left = jnp.concatenate(parts, axis=0).astype(jnp.bfloat16)
        cross = lax.dot_general(
            left, rhs_ref[f], (((1,), (1,)), ((), ())), preferred_element_type=jnp.float32
        )
        at = pl.multiple_of((step * chunk + f) * FINE, FINE)
        for i in range(a_count):
            rows = cross[i * part : (i + 1) * part]
            both = jnp.concatenate([rows[:, :width], rows[:, width:]], axis=0)
            cross_ref[pl.ds(at, FINE), i * width : (i + 1) * width] = both.astype(jnp.bfloat16)

    @pl.when(step == pl.num_programs(1) - 1)
    def _():
        low = lax.broadcasted_iota(jnp.int32, (LAGS, width), 1) < b_count
        for pair in range(a_count // 2):
            wide = jnp.dot(
                table_ref[...], cross_ref[:, 2 * pair * width : 2 * (pair + 1) * width], preferred_element_type=jnp.float32
            )
            for i in (2 * pair, 2 * pair + 1):
                both = wide[:, (i % 2) * width : (i % 2 + 1) * width]
                cos_part, sin_part = both[:LAGS], both[LAGS:]
                joined = jnp.where(
                    low,
                    cos_part + pltpu.roll(sin_part, b_count, axis=1),
                    pltpu.roll(cos_part, b_count, axis=1) - sin_part,
                )
                turned = joined.T
                at = i % ROWS * b_count
                own_ref[(i // ROWS) ^ swap_a, at : at + b_count, :] = turned[:b_count].astype(jnp.bfloat16)
                flip_ref[pl.ds(i, b_count, stride=a_count), :] = turned[b_count:]
        span = b_count // 2 * a_count
        for index in range(2):
            value = flip_ref[index * span : (index + 1) * span, :].astype(jnp.bfloat16)
            other_ref[index ^ swap_b] = value


def correlate(order, a_list, b_list, table, b_blocks, chunk=16):
    blocks, _, depth = a_list[0][0].shape
    freqs = blocks * FINE
    a_count, b_count = 2 * ROWS, 4 * ROWS
    width = 2 * b_count
    stride = 4 if b_blocks > 1 else 0

    def spec(offset, advance):
        return pl.BlockSpec((chunk, ROWS, depth), lambda j, s, *_: (s, offset + advance * j, 0))

    return pl.pallas_call(
        correlate_kernel,
        grid_spec=pltpu.PrefetchScalarGridSpec(
            num_scalar_prefetch=1,
            grid=(b_blocks, blocks // chunk),
            in_specs=[spec(o, 0) for _, o in a_list]
            + [spec(o, stride) for _, o in b_list]
            + [pl.BlockSpec((2 * LAGS, freqs), lambda j, s, *_: (0, 0))],
            out_specs=[
                pl.BlockSpec((2, ROWS * b_count, LAGS), lambda j, s, *_: (0, j, 0)),
                pl.BlockSpec((2, b_count // 2 * a_count, LAGS), lambda j, s, *_: (0, j, 0)),
            ],
            scratch_shapes=[
                pltpu.VMEM((chunk, a_count, depth), jnp.float32),
                pltpu.VMEM((chunk, 2 * width, depth), jnp.bfloat16),
                pltpu.VMEM((freqs, a_count * width), jnp.bfloat16),
                pltpu.VMEM((b_count * a_count, LAGS), jnp.float32),
            ],
        ),
        out_shape=[
            jax.ShapeDtypeStruct((2, b_blocks * ROWS * b_count, LAGS), jnp.bfloat16),
            jax.ShapeDtypeStruct((2, b_blocks * b_count // 2 * a_count, LAGS), jnp.bfloat16),
        ],
        compiler_params=pltpu.CompilerParams(
            vmem_limit_bytes=VMEM_BYTES, dimension_semantics=("arbitrary", "arbitrary")
        ),
        name="correlate",
    )(order, *[a for a, _ in a_list], *[b for b, _ in b_list], table)


def whiten_sorted(raw, own, info):
    channels, windows, width = raw.shape
    blocks, _, depth = own.shape

    def kernel(info_ref, raw_ref, own_ref, stay_ref, move_ref, new_ref, wide_ref):
        whiten_block(raw_ref, new_ref, wide_ref)

        @pl.when(info_ref[3] == 1)
        def _():
            stay_ref[...] = own_ref[...]
            move_ref[...] = new_ref[...]

        @pl.when(info_ref[3] != 1)
        def _():
            stay_ref[...] = new_ref[...]
            move_ref[...] = own_ref[...]

    shape = jax.ShapeDtypeStruct(own.shape, jnp.bfloat16)
    whole = pl.BlockSpec((blocks, ROWS, depth), lambda i, *_: (0, 0, 0))
    return pl.pallas_call(
        kernel,
        grid_spec=pltpu.PrefetchScalarGridSpec(
            num_scalar_prefetch=1,
            grid=(1,),
            in_specs=[pl.BlockSpec((ROWS, windows, width), lambda i, info_ref: (info_ref[2], 0, 0)), whole],
            out_specs=[whole, whole],
            scratch_shapes=[
                pltpu.VMEM(own.shape, jnp.bfloat16),
                pltpu.VMEM((blocks // windows * 2, ROWS * windows, windows * FINE), jnp.float32),
            ],
        ),
        out_shape=[shape, shape],
        compiler_params=pltpu.CompilerParams(vmem_limit_bytes=VMEM_BYTES),
        name="whiten_sorted",
    )(info, raw, own)


def prepare(raw, partner, members):
    channels, windows, width = raw.shape
    blocks = width // 2 // FINE
    depth = 2 * windows * FINE
    count = partner.shape[0]
    chips = count // 2

    def kernel(partner_ref, raw_ref, rank_ref, info_ref, own_ref, moves_ref, half_ref, wide_ref, sem):
        group, member = lax.axis_index("group"), lax.axis_index("member")
        low = pl.multiple_of(group % 2 * ROWS, ROWS)
        copy = pltpu.make_async_copy(raw_ref.at[pl.ds(low, ROWS)], half_ref, sem)
        copy.start()
        for index in range(count):
            moves_ref[index] = -1
        for index in range(count):

            @pl.when(moves_ref[index] < 0)
            def _():
                def walk(_, here):
                    there = partner_ref[here]
                    moves_ref[here] = 0
                    moves_ref[there] = 1
                    return there ^ 1

                lax.fori_loop(0, chips, walk, jnp.int32(index))

        target = [partner_ref[2 * chip + 1 - moves_ref[2 * chip]] // 2 for chip in range(chips)]
        rank = jnp.int32(0)
        for i in range(chips):
            for j in range(i + 1, chips):
                rank += jnp.where(target[j] < target[i], math.factorial(chips - 1 - i), 0)
        rank_ref[0] = rank
        info_ref[0] = jnp.where(member < members // 2, 1, 0)
        info_ref[1] = member % 2
        info_ref[2] = group % 2
        info_ref[3] = 1 - moves_ref[group]
        copy.wait()
        whiten_block(half_ref, own_ref, wide_ref)

    return pl.pallas_call(
        kernel,
        in_specs=[pl.BlockSpec(memory_space=pltpu.SMEM), pl.BlockSpec(memory_space=pl.ANY)],
        out_specs=[pl.BlockSpec(memory_space=pltpu.SMEM)] * 2 + [pl.BlockSpec(memory_space=pltpu.VMEM)],
        out_shape=[
            jax.ShapeDtypeStruct((1,), jnp.int32),
            jax.ShapeDtypeStruct((4,), jnp.int32),
            jax.ShapeDtypeStruct((blocks, ROWS, depth), jnp.bfloat16),
        ],
        scratch_shapes=[
            pltpu.SMEM((count,), jnp.int32),
            pltpu.VMEM((ROWS, windows, width), jnp.bfloat16),
            pltpu.VMEM((blocks // windows * 2, ROWS * windows, windows * FINE), jnp.float32),
            pltpu.SemaphoreType.DMA(()),
        ],
        compiler_params=pltpu.CompilerParams(vmem_limit_bytes=VMEM_BYTES),
        name="prepare",
    )(pltpu.with_memory_space_constraint(partner, pltpu.HBM), pltpu.with_memory_space_constraint(raw, pltpu.HBM))


def choose(info, pieces):
    shape = pieces[0].shape

    def kernel(info_ref, far_ref, near_ref, here_ref, there_ref, out_ref, sems):
        def run(first, second):
            copies = [
                pltpu.make_async_copy(ref, out_ref.at[index], sems.at[index])
                for index, ref in enumerate((first, second))
            ]
            for copy in copies:
                copy.start()
            for copy in copies:
                copy.wait()

        @pl.when(info_ref[3] == 1)
        def _():
            run(here_ref, there_ref)

        @pl.when(info_ref[3] != 1)
        def _():
            run(far_ref, near_ref)

    return pl.pallas_call(
        kernel,
        in_specs=[pl.BlockSpec(memory_space=pltpu.SMEM)] + [pl.BlockSpec(memory_space=pl.ANY)] * 4,
        out_specs=pl.BlockSpec(memory_space=pltpu.VMEM),
        out_shape=jax.ShapeDtypeStruct((2,) + shape, jnp.bfloat16),
        scratch_shapes=[pltpu.SemaphoreType.DMA((2,))],
        compiler_params=pltpu.CompilerParams(vmem_limit_bytes=VMEM_BYTES),
        name="choose",
    )(info, *pieces)


def place(info, pieces, members, whole=None):
    others = 2 * members * ROWS
    half = others // 2
    rest = () if whole is None else (whole,)

    def kernel(info_ref, *refs):
        out_ref, sems = refs[-2:]
        odd, core = info_ref[1], info_ref[2]
        if whole is None:
            which = core
            far_ref, near_ref, here_ref, there_ref = refs[:4]
        else:
            which = 1 - core
            far_ref, near_ref = here_ref, there_ref = refs[0].at[0], refs[0].at[1]

        def run(copies):
            copies = [pltpu.make_async_copy(*copy, sems.at[index]) for index, copy in enumerate(copies)]
            for copy in copies:
                copy.start()
            for copy in copies:
                copy.wait()

        def put_stay(side, ref):
            low = pl.multiple_of(which * ROWS, ROWS)
            at = pl.multiple_of(side * half, half)
            return [(ref.reshape(ROWS, half, LAGS), out_ref.at[pl.ds(low, ROWS), pl.ds(at, half), :])]

        def put_move(side, ref):
            source = ref.reshape(2 * ROWS, 2 * ROWS, LAGS)
            copies = []
            for shard in range(2):
                at = pl.multiple_of(side * half + shard * 2 * ROWS + which * ROWS, ROWS)
                copies.append((source.at[:, pl.ds(shard * ROWS, ROWS), :], out_ref.at[:, pl.ds(at, ROWS), :]))
            return copies

        @pl.when(info_ref[3] == 1)
        def _():
            run(put_stay(1 - odd, far_ref) + put_stay(odd, near_ref))

        @pl.when(info_ref[3] != 1)
        def _():
            run(put_move(odd, here_ref) + put_move(1 - odd, there_ref))

    return pl.pallas_call(
        kernel,
        in_specs=[pl.BlockSpec(memory_space=pltpu.SMEM)]
        + [pl.BlockSpec(memory_space=pltpu.VMEM)] * len(pieces)
        + [pl.BlockSpec(memory_space=pl.ANY)] * len(rest),
        out_specs=pl.BlockSpec(memory_space=pl.ANY),
        out_shape=jax.ShapeDtypeStruct((2 * ROWS, others, LAGS), jnp.bfloat16),
        scratch_shapes=[pltpu.SemaphoreType.DMA((4,))],
        input_output_aliases={1 + len(pieces): 0} if rest else {},
        compiler_params=pltpu.CompilerParams(vmem_limit_bytes=VMEM_BYTES),
        name="place",
    )(info, *pieces, *rest)


def permute(value, groups, members, target):
    pairs = []
    for group, member in itertools.product(range(groups), range(members)):
        to_group, to_member = target(group, member)
        pairs.append((group * members + member, to_group * members + to_member))
    return lax.ppermute(value, ("group", "member"), pairs)


def on_device_any(spectra, partner):
    group_count = lax.axis_size("group")
    channels, windows, width = spectra.shape
    white = whiten(spectra)
    blocks, _, depth = white.shape
    spread = lax.all_to_all(white, "group", split_axis=1, concat_axis=1, tiled=True)
    shares = spread.reshape(blocks, group_count, channels // group_count, depth)
    ordered = jnp.take(shares, partner, axis=1).reshape(white.shape)
    arrived = lax.all_to_all(ordered, "group", split_axis=1, concat_axis=1, tiled=True)
    theirs = lax.all_gather(arrived, "member", axis=1, tiled=True)
    table = jnp.asarray(lag_rows(width // 2, windows))
    others = theirs.shape[1]
    order = jnp.zeros((3,), jnp.int32)
    result, _ = correlate(
        order, [(white, 0), (white, 1)], [(theirs, q) for q in range(4)], table, others // (4 * ROWS)
    )
    result = result.reshape(2, others // (4 * ROWS), ROWS, 4 * ROWS, LAGS)
    return jnp.transpose(result, (0, 2, 1, 3, 4)).reshape(channels, others, LAGS)


def on_device_pairs(spectra, partner):
    groups, members = lax.axis_size("group"), lax.axis_size("member")
    chips = groups // 2
    windows, width = spectra.shape[1:]

    def across(value):
        return permute(value, groups, members, lambda g, m: (g ^ 1, m))

    other_raw = across(spectra)
    rank, info, own = prepare(spectra, partner, members)
    stay, move = whiten_sorted(other_raw, own, info)

    far = (2, 0, 3, 1)
    back = tuple(far.index(m) for m in range(members))
    near = (0, 2, 1, 3)
    orders = list(itertools.permutations(range(chips)))

    def straight_way(order):
        return sum(order[chip] == chips - 1 - chip for chip in range(chips)) < 2

    def go(order):
        def branch(stay, move):
            def go_on(value, flip):
                return permute(value, groups, members, lambda g, m: (2 * order[g // 2] + g % 2, m ^ flip))

            here = go_on(move, 0)
            first = permute(stay, groups, members, lambda g, m: (g, far[m]))
            if straight_way(order):
                there = go_on(move, 1)
            else:
                barred, _, stay = lax.optimization_barrier((here, first, stay))
                there = permute(barred, groups, members, lambda g, m: (g, m ^ 1))
            second = permute(stay, groups, members, lambda g, m: (g, near[m]))
            return first, second, here, across(here), there, across(there)

        return branch

    def home(order):
        def branch(first, second, same, other):
            def back_home(value, flip):
                return permute(value, groups, members, lambda g, m: (2 * order.index(g // 2) + g % 2, m ^ flip))

            here = back_home(same, 0)
            from_near = permute(second, groups, members, lambda g, m: (g, near[m]))
            if straight_way(order):
                there = back_home(other, 1)
            else:
                swapped = permute(other, groups, members, lambda g, m: (g, m ^ 1))
                first, swapped, _, _ = lax.optimization_barrier((first, swapped, from_near, here))
                there = back_home(swapped, 0)
            from_far = permute(first, groups, members, lambda g, m: (g, back[m]))
            return from_far, from_near, here, there

        return branch

    first, second, here, here_too, there, there_too = lax.switch(
        rank[0], [go(order) for order in orders], stay, move
    )
    table = jnp.asarray(lag_rows(width // 2, windows))
    straight, mirrored = correlate(
        info,
        [(first, 0), (second, 0)],
        [(here, 0), (here_too, 0), (there, 0), (there_too, 0)],
        table,
        1,
    )
    pieces = lax.switch(
        rank[0], [home(order) for order in orders], straight[0], straight[1], mirrored[0], mirrored[1]
    )
    got = across(choose(info, pieces))
    return place(info, (got,), members, place(info, pieces, members))


def solution(mesh):
    placed = (P(("group", "member"), None, None), P())
    small = mesh.shape["group"] <= 8 and mesh.shape["member"] == 4
    return jax.shard_map(
        on_device_pairs if small else on_device_any,
        mesh=mesh,
        in_specs=placed,
        out_specs=P(("group", "member"), None, None),
        check_vma=False,
    )
```

```python
import itertools
import math

import jax
import jax.numpy as jnp
import ml_dtypes
import numpy as np
from jax import lax
from jax.experimental import pallas as pl
from jax.experimental.pallas import tpu as pltpu
from jax.sharding import PartitionSpec as P

LAGS = 128
HALF = 64
FINE = 16
ROWS = 16
VMEM_BYTES = 48 * 1024 * 1024


def lag_rows(freq_count, window_count):
    lag = np.arange(LAGS) - LAGS // 2
    freq = np.arange(freq_count)
    angle = np.pi * np.mod(lag[:, None] * freq[None, :], 2 * freq_count) / freq_count
    norm = 1.0 / math.sqrt(window_count * freq_count)
    rows = np.concatenate([np.cos(angle), -np.sin(angle)], axis=0) * norm
    return rows.astype(np.float32).astype(ml_dtypes.bfloat16)


def whiten_block(raw_ref, out_ref, wide_ref):
    rows, windows, width = raw_ref.shape
    freqs = width // 2
    lanes = windows * FINE
    groups = freqs // lanes
    for slab in range(2 * groups):
        value = raw_ref[:, :, slab * lanes : (slab + 1) * lanes].astype(jnp.float32)
        wide_ref[slab] = value.reshape(rows * windows, lanes)

    def window(slab, w):
        return wide_ref[slab, pl.ds(w, rows, stride=windows), :]

    pieces = []
    for group in range(groups):
        piece = jnp.zeros((rows, lanes), jnp.float32)
        for w in range(windows):
            real, imag = window(group, w), window(groups + group, w)
            piece += real * real + imag * imag
        pieces.append(piece)
    power = jnp.concatenate(pieces, axis=1)
    edge = jnp.zeros((rows, 2 * HALF), jnp.float32)
    padded = jnp.concatenate([edge, power, edge], axis=1)
    total = padded
    length = padded.shape[1]
    step = 1
    while step < 2 * HALF:
        total = total + pltpu.roll(total, length - step, axis=1)
        step *= 2
    total = total + pltpu.roll(padded, length - 2 * HALF, axis=1)
    smoothed = pltpu.roll(total, length - HALF, axis=1)[:, :freqs]
    place = lax.broadcasted_iota(jnp.int32, (rows, freqs), 1)
    counts = jnp.minimum(place + HALF, freqs - 1) - jnp.maximum(place - HALF, 0) + 1
    average = smoothed / (counts.astype(jnp.float32) * windows)
    factor = 1.0 / jnp.sqrt(average + 1e-05)
    granule = lax.broadcasted_iota(jnp.int32, (rows, lanes), 1) // FINE
    for part in range(2):
        for group in range(groups):
            scale = factor[:, group * lanes : (group + 1) * lanes]
            items = [window(part * groups + group, w) * scale for w in range(windows)]
            dist = windows // 2
            while dist:
                keep = (granule & dist) == 0
                nxt = list(items)
                for i in range(windows):
                    if i & dist:
                        continue
                    j = i + dist
                    nxt[i] = jnp.where(keep, items[i], pltpu.roll(items[j], dist * FINE, axis=1))
                    nxt[j] = jnp.where(keep, pltpu.roll(items[i], lanes - dist * FINE, axis=1), items[j])
                items = nxt
                dist //= 2
            for i in range(windows):
                out_ref[group * windows + i, :, part * lanes : (part + 1) * lanes] = items[i].astype(jnp.bfloat16)


def whiten(raw):
    channels, windows, width = raw.shape
    blocks = width // 2 // FINE
    return pl.pallas_call(
        whiten_block,
        grid=(channels // ROWS,),
        in_specs=[pl.BlockSpec((ROWS, windows, width), lambda i: (i, 0, 0))],
        out_specs=pl.BlockSpec((blocks, ROWS, 2 * windows * FINE), lambda i: (0, i, 0)),
        out_shape=jax.ShapeDtypeStruct((blocks, channels, 2 * windows * FINE), jnp.bfloat16),
        scratch_shapes=[pltpu.VMEM((blocks // windows * 2, ROWS * windows, windows * FINE), jnp.float32)],
        compiler_params=pltpu.CompilerParams(vmem_limit_bytes=VMEM_BYTES),
        name="whiten",
    )(raw)


def correlate_kernel(order_ref, a1, a2, b1, b2, b3, b4, table_ref, own_ref, other_ref, rows_ref, rhs_ref, cross_ref, flip_ref):
    step = pl.program_id(1)
    chunk, _, depth = a1.shape
    half = depth // 2
    a_count = 2 * ROWS
    b_count = 4 * ROWS
    width = 2 * b_count
    swap_a, swap_b, first_half = order_ref[0], order_ref[1], order_ref[2]
    part = FINE // 2
    lane = lax.broadcasted_iota(jnp.int32, (part, depth), 1)
    mask = (lane % part == lax.broadcasted_iota(jnp.int32, (part, depth), 0)).astype(jnp.float32)
    upper = (lax.broadcasted_iota(jnp.int32, (ROWS, depth), 1) // part % 2).astype(jnp.float32)
    upper = upper.astype(jnp.bfloat16)
    sides = (1 - upper, upper)

    for index, ref in enumerate((a1, a2)):
        at = pl.multiple_of((index ^ swap_a) * ROWS, ROWS)
        for f in range(chunk):
            rows_ref[f, pl.ds(at, ROWS), :] = ref[f].astype(jnp.float32)
    for index, ref in enumerate((b1, b2, b3, b4)):
        spot = ((index // 2) ^ swap_b) * 2 + ((index % 2) ^ first_half)
        at = pl.multiple_of(spot * ROWS, ROWS)
        for f in range(chunk):
            value = ref[f]
            turned = jnp.concatenate([-value[:, half:], value[:, :half]], axis=1)
            for side in range(2):
                rhs_ref[f, pl.ds(side * width + at, ROWS), :] = value * sides[side]
                rhs_ref[f, pl.ds(side * width + b_count + at, ROWS), :] = turned * sides[side]
    for f in range(chunk):
        parts = []
        for i in range(a_count):
            parts.append(jnp.broadcast_to(rows_ref[f, i : i + 1, :], (part, depth)) * mask)
        left = jnp.concatenate(parts, axis=0).astype(jnp.bfloat16)
        cross = lax.dot_general(
            left, rhs_ref[f], (((1,), (1,)), ((), ())), preferred_element_type=jnp.float32
        )
        at = pl.multiple_of((step * chunk + f) * FINE, FINE)
        for i in range(a_count):
            rows = cross[i * part : (i + 1) * part]
            both = jnp.concatenate([rows[:, :width], rows[:, width:]], axis=0)
            cross_ref[pl.ds(at, FINE), i * width : (i + 1) * width] = both.astype(jnp.bfloat16)

    @pl.when(step == pl.num_programs(1) - 1)
    def _():
        low = lax.broadcasted_iota(jnp.int32, (LAGS, width), 1) < b_count
        for pair in range(a_count // 2):
            wide = jnp.dot(
                table_ref[...], cross_ref[:, 2 * pair * width : 2 * (pair + 1) * width], preferred_element_type=jnp.float32
            )
            for i in (2 * pair, 2 * pair + 1):
                both = wide[:, (i % 2) * width : (i % 2 + 1) * width]
                cos_part, sin_part = both[:LAGS], both[LAGS:]
                joined = jnp.where(
                    low,
                    cos_part + pltpu.roll(sin_part, b_count, axis=1),
                    pltpu.roll(cos_part, b_count, axis=1) - sin_part,
                )
                turned = joined.T
                at = i % ROWS * b_count
                own_ref[(i // ROWS) ^ swap_a, at : at + b_count, :] = turned[:b_count].astype(jnp.bfloat16)
                flip_ref[pl.ds(i, b_count, stride=a_count), :] = turned[b_count:]
        span = b_count // 2 * a_count
        for index in range(2):
            value = flip_ref[index * span : (index + 1) * span, :].astype(jnp.bfloat16)
            other_ref[index ^ swap_b] = value


def correlate(order, a_list, b_list, table, b_blocks, chunk=16):
    blocks, _, depth = a_list[0][0].shape
    freqs = blocks * FINE
    a_count, b_count = 2 * ROWS, 4 * ROWS
    width = 2 * b_count
    stride = 4 if b_blocks > 1 else 0

    def spec(offset, advance):
        return pl.BlockSpec((chunk, ROWS, depth), lambda j, s, *_: (s, offset + advance * j, 0))

    return pl.pallas_call(
        correlate_kernel,
        grid_spec=pltpu.PrefetchScalarGridSpec(
            num_scalar_prefetch=1,
            grid=(b_blocks, blocks // chunk),
            in_specs=[spec(o, 0) for _, o in a_list]
            + [spec(o, stride) for _, o in b_list]
            + [pl.BlockSpec((2 * LAGS, freqs), lambda j, s, *_: (0, 0))],
            out_specs=[
                pl.BlockSpec((2, ROWS * b_count, LAGS), lambda j, s, *_: (0, j, 0)),
                pl.BlockSpec((2, b_count // 2 * a_count, LAGS), lambda j, s, *_: (0, j, 0)),
            ],
            scratch_shapes=[
                pltpu.VMEM((chunk, a_count, depth), jnp.float32),
                pltpu.VMEM((chunk, 2 * width, depth), jnp.bfloat16),
                pltpu.VMEM((freqs, a_count * width), jnp.bfloat16),
                pltpu.VMEM((b_count * a_count, LAGS), jnp.float32),
            ],
        ),
        out_shape=[
            jax.ShapeDtypeStruct((2, b_blocks * ROWS * b_count, LAGS), jnp.bfloat16),
            jax.ShapeDtypeStruct((2, b_blocks * b_count // 2 * a_count, LAGS), jnp.bfloat16),
        ],
        compiler_params=pltpu.CompilerParams(
            vmem_limit_bytes=VMEM_BYTES, dimension_semantics=("arbitrary", "arbitrary")
        ),
        name="correlate",
    )(order, *[a for a, _ in a_list], *[b for b, _ in b_list], table)


def whiten_sorted(raw, own, info):
    windows, width = raw.shape[1:]
    blocks = own.shape[0]

    def kernel(info_ref, raw_ref, own_ref, stay_ref, move_ref, wide_ref):
        low = pl.multiple_of(info_ref[2] * ROWS, ROWS)
        half_ref = raw_ref.at[pl.ds(low, ROWS)]

        @pl.when(info_ref[3] == 1)
        def _():
            stay_ref[...] = own_ref[...]
            whiten_block(half_ref, move_ref, wide_ref)

        @pl.when(info_ref[3] != 1)
        def _():
            move_ref[...] = own_ref[...]
            whiten_block(half_ref, stay_ref, wide_ref)

    shape = jax.ShapeDtypeStruct(own.shape, jnp.bfloat16)
    return pl.pallas_call(
        kernel,
        in_specs=[pl.BlockSpec(memory_space=pltpu.SMEM)] + [pl.BlockSpec(memory_space=pltpu.VMEM)] * 2,
        out_specs=[pl.BlockSpec(memory_space=pltpu.VMEM)] * 2,
        out_shape=[shape, shape],
        scratch_shapes=[pltpu.VMEM((blocks // windows * 2, ROWS * windows, windows * FINE), jnp.float32)],
        compiler_params=pltpu.CompilerParams(vmem_limit_bytes=VMEM_BYTES),
        name="whiten_sorted",
    )(info, raw, own)


def prepare(raw, partner, members):
    channels, windows, width = raw.shape
    blocks = width // 2 // FINE
    depth = 2 * windows * FINE
    count = partner.shape[0]
    chips = count // 2

    def kernel(partner_ref, raw_ref, rank_ref, info_ref, own_ref, moves_ref, half_ref, wide_ref, sem):
        group, member = lax.axis_index("group"), lax.axis_index("member")
        low = pl.multiple_of(group % 2 * ROWS, ROWS)
        copy = pltpu.make_async_copy(raw_ref.at[pl.ds(low, ROWS)], half_ref, sem)
        copy.start()
        for index in range(count):
            moves_ref[index] = -1
        for index in range(count):

            @pl.when(moves_ref[index] < 0)
            def _():
                def walk(_, here):
                    there = partner_ref[here]
                    moves_ref[here] = 0
                    moves_ref[there] = 1
                    return there ^ 1

                lax.fori_loop(0, chips, walk, jnp.int32(index))

        target = [partner_ref[2 * chip + 1 - moves_ref[2 * chip]] // 2 for chip in range(chips)]
        rank = jnp.int32(0)
        for i in range(chips):
            for j in range(i + 1, chips):
                rank += jnp.where(target[j] < target[i], math.factorial(chips - 1 - i), 0)
        rank_ref[0] = rank
        info_ref[0] = jnp.where(member < members // 2, 1, 0)
        info_ref[1] = member % 2
        info_ref[2] = group % 2
        info_ref[3] = 1 - moves_ref[group]
        copy.wait()
        whiten_block(half_ref, own_ref, wide_ref)

    return pl.pallas_call(
        kernel,
        in_specs=[pl.BlockSpec(memory_space=pltpu.SMEM), pl.BlockSpec(memory_space=pl.ANY)],
        out_specs=[pl.BlockSpec(memory_space=pltpu.SMEM)] * 2 + [pl.BlockSpec(memory_space=pltpu.VMEM)],
        out_shape=[
            jax.ShapeDtypeStruct((1,), jnp.int32),
            jax.ShapeDtypeStruct((4,), jnp.int32),
            jax.ShapeDtypeStruct((blocks, ROWS, depth), jnp.bfloat16),
        ],
        scratch_shapes=[
            pltpu.SMEM((count,), jnp.int32),
            pltpu.VMEM((ROWS, windows, width), jnp.bfloat16),
            pltpu.VMEM((blocks // windows * 2, ROWS * windows, windows * FINE), jnp.float32),
            pltpu.SemaphoreType.DMA(()),
        ],
        compiler_params=pltpu.CompilerParams(vmem_limit_bytes=VMEM_BYTES),
        name="prepare",
    )(pltpu.with_memory_space_constraint(partner, pltpu.HBM), pltpu.with_memory_space_constraint(raw, pltpu.HBM))


def choose(info, pieces):
    shape = pieces[0].shape

    def kernel(info_ref, far_ref, near_ref, here_ref, there_ref, out_ref, sems):
        def run(first, second):
            copies = [
                pltpu.make_async_copy(ref, out_ref.at[index], sems.at[index])
                for index, ref in enumerate((first, second))
            ]
            for copy in copies:
                copy.start()
            for copy in copies:
                copy.wait()

        @pl.when(info_ref[3] == 1)
        def _():
            run(here_ref, there_ref)

        @pl.when(info_ref[3] != 1)
        def _():
            run(far_ref, near_ref)

    return pl.pallas_call(
        kernel,
        in_specs=[pl.BlockSpec(memory_space=pltpu.SMEM)] + [pl.BlockSpec(memory_space=pl.ANY)] * 4,
        out_specs=pl.BlockSpec(memory_space=pltpu.VMEM),
        out_shape=jax.ShapeDtypeStruct((2,) + shape, jnp.bfloat16),
        scratch_shapes=[pltpu.SemaphoreType.DMA((2,))],
        compiler_params=pltpu.CompilerParams(vmem_limit_bytes=VMEM_BYTES),
        name="choose",
    )(info, *pieces)


def place(info, pieces, members, whole=None):
    others = 2 * members * ROWS
    half = others // 2
    rest = () if whole is None else (whole,)

    def kernel(info_ref, *refs):
        out_ref, sems = refs[-2:]
        odd, core = info_ref[1], info_ref[2]
        if whole is None:
            which = core
            far_ref, near_ref, here_ref, there_ref = refs[:4]
        else:
            which = 1 - core
            far_ref, near_ref = here_ref, there_ref = refs[0].at[0], refs[0].at[1]

        def run(copies):
            copies = [pltpu.make_async_copy(*copy, sems.at[index]) for index, copy in enumerate(copies)]
            for copy in copies:
                copy.start()
            for copy in copies:
                copy.wait()

        def put_stay(side, ref):
            low = pl.multiple_of(which * ROWS, ROWS)
            at = pl.multiple_of(side * half, half)
            return [(ref.reshape(ROWS, half, LAGS), out_ref.at[pl.ds(low, ROWS), pl.ds(at, half), :])]

        def put_move(side, ref):
            source = ref.reshape(2 * ROWS, 2 * ROWS, LAGS)
            copies = []
            for shard in range(2):
                at = pl.multiple_of(side * half + shard * 2 * ROWS + which * ROWS, ROWS)
                copies.append((source.at[:, pl.ds(shard * ROWS, ROWS), :], out_ref.at[:, pl.ds(at, ROWS), :]))
            return copies

        @pl.when(info_ref[3] == 1)
        def _():
            run(put_stay(1 - odd, far_ref) + put_stay(odd, near_ref))

        @pl.when(info_ref[3] != 1)
        def _():
            run(put_move(odd, here_ref) + put_move(1 - odd, there_ref))

    return pl.pallas_call(
        kernel,
        in_specs=[pl.BlockSpec(memory_space=pltpu.SMEM)]
        + [pl.BlockSpec(memory_space=pltpu.VMEM)] * len(pieces)
        + [pl.BlockSpec(memory_space=pl.ANY)] * len(rest),
        out_specs=pl.BlockSpec(memory_space=pl.ANY),
        out_shape=jax.ShapeDtypeStruct((2 * ROWS, others, LAGS), jnp.bfloat16),
        scratch_shapes=[pltpu.SemaphoreType.DMA((4,))],
        input_output_aliases={1 + len(pieces): 0} if rest else {},
        compiler_params=pltpu.CompilerParams(vmem_limit_bytes=VMEM_BYTES),
        name="place",
    )(info, *pieces, *rest)


def permute(value, groups, members, target):
    pairs = []
    for group, member in itertools.product(range(groups), range(members)):
        to_group, to_member = target(group, member)
        pairs.append((group * members + member, to_group * members + to_member))
    return lax.ppermute(value, ("group", "member"), pairs)


def on_device_any(spectra, partner):
    group_count = lax.axis_size("group")
    channels, windows, width = spectra.shape
    white = whiten(spectra)
    blocks, _, depth = white.shape
    spread = lax.all_to_all(white, "group", split_axis=1, concat_axis=1, tiled=True)
    shares = spread.reshape(blocks, group_count, channels // group_count, depth)
    ordered = jnp.take(shares, partner, axis=1).reshape(white.shape)
    arrived = lax.all_to_all(ordered, "group", split_axis=1, concat_axis=1, tiled=True)
    theirs = lax.all_gather(arrived, "member", axis=1, tiled=True)
    table = jnp.asarray(lag_rows(width // 2, windows))
    others = theirs.shape[1]
    order = jnp.zeros((3,), jnp.int32)
    result, _ = correlate(
        order, [(white, 0), (white, 1)], [(theirs, q) for q in range(4)], table, others // (4 * ROWS)
    )
    result = result.reshape(2, others // (4 * ROWS), ROWS, 4 * ROWS, LAGS)
    return jnp.transpose(result, (0, 2, 1, 3, 4)).reshape(channels, others, LAGS)


def on_device_pairs(spectra, partner):
    groups, members = lax.axis_size("group"), lax.axis_size("member")
    chips = groups // 2
    windows, width = spectra.shape[1:]

    def across(value):
        return permute(value, groups, members, lambda g, m: (g ^ 1, m))

    other_raw = across(spectra)
    rank, info, own = prepare(spectra, partner, members)
    stay, move = whiten_sorted(other_raw, own, info)

    far = (2, 0, 3, 1)
    back = tuple(far.index(m) for m in range(members))
    near = (0, 2, 1, 3)
    orders = list(itertools.permutations(range(chips)))

    def straight_way(order):
        return sum(order[chip] == chips - 1 - chip for chip in range(chips)) < 2

    def go(order):
        def branch(stay, move):
            def go_on(value, flip):
                return permute(value, groups, members, lambda g, m: (2 * order[g // 2] + g % 2, m ^ flip))

            here = go_on(move, 0)
            first = permute(stay, groups, members, lambda g, m: (g, far[m]))
            if straight_way(order):
                there = go_on(move, 1)
            else:
                there = permute(here, groups, members, lambda g, m: (g, m ^ 1))
                _, stay = lax.optimization_barrier((first, stay))
            second = permute(stay, groups, members, lambda g, m: (g, near[m]))
            return first, second, here, across(here), there, across(there)

        return branch

    def home(order):
        def branch(first, second, same, other):
            def back_home(value, flip):
                return permute(value, groups, members, lambda g, m: (2 * order.index(g // 2) + g % 2, m ^ flip))

            here = back_home(same, 0)
            from_near = permute(second, groups, members, lambda g, m: (g, near[m]))
            if straight_way(order):
                there = back_home(other, 1)
            else:
                swapped = permute(other, groups, members, lambda g, m: (g, m ^ 1))
                first, swapped, _, _ = lax.optimization_barrier((first, swapped, from_near, here))
                there = back_home(swapped, 0)
            from_far = permute(first, groups, members, lambda g, m: (g, back[m]))
            return from_far, from_near, here, there

        return branch

    first, second, here, here_too, there, there_too = lax.switch(
        rank[0], [go(order) for order in orders], stay, move
    )
    table = jnp.asarray(lag_rows(width // 2, windows))
    straight, mirrored = correlate(
        info,
        [(first, 0), (second, 0)],
        [(here, 0), (here_too, 0), (there, 0), (there_too, 0)],
        table,
        1,
    )
    pieces = lax.switch(
        rank[0], [home(order) for order in orders], straight[0], straight[1], mirrored[0], mirrored[1]
    )
    got = across(choose(info, pieces))
    return place(info, (got,), members, place(info, pieces, members))


def solution(mesh):
    placed = (P(("group", "member"), None, None), P())
    small = mesh.shape["group"] <= 8 and mesh.shape["member"] == 4
    return jax.shard_map(
        on_device_pairs if small else on_device_any,
        mesh=mesh,
        in_specs=placed,
        out_specs=P(("group", "member"), None, None),
        check_vma=False,
    )
```

```python
import itertools
import math

import jax
import jax.numpy as jnp
import ml_dtypes
import numpy as np
from jax import lax
from jax.experimental import pallas as pl
from jax.experimental.pallas import tpu as pltpu
from jax.sharding import PartitionSpec as P

LAGS = 128
HALF = 64
FINE = 16
ROWS = 16
VMEM_BYTES = 48 * 1024 * 1024


def lag_rows(freq_count, window_count):
    lag = np.arange(LAGS) - LAGS // 2
    freq = np.arange(freq_count)
    angle = np.pi * np.mod(lag[:, None] * freq[None, :], 2 * freq_count) / freq_count
    norm = 1.0 / math.sqrt(window_count * freq_count)
    rows = np.concatenate([np.cos(angle), -np.sin(angle)], axis=0) * norm
    return rows.astype(np.float32).astype(ml_dtypes.bfloat16)


def whiten_block(raw_ref, out_ref, wide_ref):
    rows, windows, width = raw_ref.shape
    freqs = width // 2
    lanes = windows * FINE
    groups = freqs // lanes
    for slab in range(2 * groups):
        value = raw_ref[:, :, slab * lanes : (slab + 1) * lanes].astype(jnp.float32)
        wide_ref[slab] = value.reshape(rows * windows, lanes)

    def window(slab, w):
        return wide_ref[slab, pl.ds(w, rows, stride=windows), :]

    pieces = []
    for group in range(groups):
        piece = jnp.zeros((rows, lanes), jnp.float32)
        for w in range(windows):
            real, imag = window(group, w), window(groups + group, w)
            piece += real * real + imag * imag
        pieces.append(piece)
    power = jnp.concatenate(pieces, axis=1)
    edge = jnp.zeros((rows, 2 * HALF), jnp.float32)
    padded = jnp.concatenate([edge, power, edge], axis=1)
    total = padded
    length = padded.shape[1]
    step = 1
    while step < 2 * HALF:
        total = total + pltpu.roll(total, length - step, axis=1)
        step *= 2
    total = total + pltpu.roll(padded, length - 2 * HALF, axis=1)
    smoothed = pltpu.roll(total, length - HALF, axis=1)[:, :freqs]
    place = lax.broadcasted_iota(jnp.int32, (rows, freqs), 1)
    counts = jnp.minimum(place + HALF, freqs - 1) - jnp.maximum(place - HALF, 0) + 1
    average = smoothed / (counts.astype(jnp.float32) * windows)
    factor = 1.0 / jnp.sqrt(average + 1e-05)
    granule = lax.broadcasted_iota(jnp.int32, (rows, lanes), 1) // FINE
    for part in range(2):
        for group in range(groups):
            scale = factor[:, group * lanes : (group + 1) * lanes]
            items = [window(part * groups + group, w) * scale for w in range(windows)]
            dist = windows // 2
            while dist:
                keep = (granule & dist) == 0
                nxt = list(items)
                for i in range(windows):
                    if i & dist:
                        continue
                    j = i + dist
                    nxt[i] = jnp.where(keep, items[i], pltpu.roll(items[j], dist * FINE, axis=1))
                    nxt[j] = jnp.where(keep, pltpu.roll(items[i], lanes - dist * FINE, axis=1), items[j])
                items = nxt
                dist //= 2
            for i in range(windows):
                out_ref[group * windows + i, :, part * lanes : (part + 1) * lanes] = items[i].astype(jnp.bfloat16)


def whiten(raw):
    channels, windows, width = raw.shape
    blocks = width // 2 // FINE
    return pl.pallas_call(
        whiten_block,
        grid=(channels // ROWS,),
        in_specs=[pl.BlockSpec((ROWS, windows, width), lambda i: (i, 0, 0))],
        out_specs=pl.BlockSpec((blocks, ROWS, 2 * windows * FINE), lambda i: (0, i, 0)),
        out_shape=jax.ShapeDtypeStruct((blocks, channels, 2 * windows * FINE), jnp.bfloat16),
        scratch_shapes=[pltpu.VMEM((blocks // windows * 2, ROWS * windows, windows * FINE), jnp.float32)],
        compiler_params=pltpu.CompilerParams(vmem_limit_bytes=VMEM_BYTES),
        name="whiten",
    )(raw)


def correlate_kernel(order_ref, a1, a2, b1, b2, b3, b4, table_ref, own_ref, other_ref, rows_ref, rhs_ref, cross_ref, flip_ref):
    step = pl.program_id(1)
    chunk, _, depth = a1.shape
    half = depth // 2
    a_count = 2 * ROWS
    b_count = 4 * ROWS
    width = 2 * b_count
    swap_a, swap_b, first_half = order_ref[0], order_ref[1], order_ref[2]
    part = FINE // 2
    lane = lax.broadcasted_iota(jnp.int32, (part, depth), 1)
    mask = (lane % part == lax.broadcasted_iota(jnp.int32, (part, depth), 0)).astype(jnp.float32)
    upper = (lax.broadcasted_iota(jnp.int32, (ROWS, depth), 1) // part % 2).astype(jnp.float32)
    upper = upper.astype(jnp.bfloat16)
    sides = (1 - upper, upper)

    for index, ref in enumerate((a1, a2)):
        at = pl.multiple_of((index ^ swap_a) * ROWS, ROWS)
        for f in range(chunk):
            rows_ref[f, pl.ds(at, ROWS), :] = ref[f].astype(jnp.float32)
    for index, ref in enumerate((b1, b2, b3, b4)):
        spot = ((index // 2) ^ swap_b) * 2 + ((index % 2) ^ first_half)
        at = pl.multiple_of(spot * ROWS, ROWS)
        for f in range(chunk):
            value = ref[f]
            turned = jnp.concatenate([-value[:, half:], value[:, :half]], axis=1)
            for side in range(2):
                rhs_ref[f, pl.ds(side * width + at, ROWS), :] = value * sides[side]
                rhs_ref[f, pl.ds(side * width + b_count + at, ROWS), :] = turned * sides[side]
    for f in range(chunk):
        parts = []
        for i in range(a_count):
            parts.append(jnp.broadcast_to(rows_ref[f, i : i + 1, :], (part, depth)) * mask)
        left = jnp.concatenate(parts, axis=0).astype(jnp.bfloat16)
        cross = lax.dot_general(
            left, rhs_ref[f], (((1,), (1,)), ((), ())), preferred_element_type=jnp.float32
        )
        at = pl.multiple_of((step * chunk + f) * FINE, FINE)
        for i in range(a_count):
            rows = cross[i * part : (i + 1) * part]
            both = jnp.concatenate([rows[:, :width], rows[:, width:]], axis=0)
            cross_ref[pl.ds(at, FINE), i * width : (i + 1) * width] = both.astype(jnp.bfloat16)

    @pl.when(step == pl.num_programs(1) - 1)
    def _():
        low = lax.broadcasted_iota(jnp.int32, (LAGS, width), 1) < b_count
        for pair in range(a_count // 2):
            wide = jnp.dot(
                table_ref[...], cross_ref[:, 2 * pair * width : 2 * (pair + 1) * width], preferred_element_type=jnp.float32
            )
            for i in (2 * pair, 2 * pair + 1):
                both = wide[:, (i % 2) * width : (i % 2 + 1) * width]
                cos_part, sin_part = both[:LAGS], both[LAGS:]
                joined = jnp.where(
                    low,
                    cos_part + pltpu.roll(sin_part, b_count, axis=1),
                    pltpu.roll(cos_part, b_count, axis=1) - sin_part,
                )
                turned = joined.T
                at = i % ROWS * b_count
                own_ref[(i // ROWS) ^ swap_a, at : at + b_count, :] = turned[:b_count].astype(jnp.bfloat16)
                flip_ref[pl.ds(i, b_count, stride=a_count), :] = turned[b_count:]
        span = b_count // 2 * a_count
        for index in range(2):
            value = flip_ref[index * span : (index + 1) * span, :].astype(jnp.bfloat16)
            other_ref[index ^ swap_b] = value


def correlate(order, a_list, b_list, table, b_blocks, chunk=32):
    blocks, _, depth = a_list[0][0].shape
    freqs = blocks * FINE
    a_count, b_count = 2 * ROWS, 4 * ROWS
    width = 2 * b_count
    stride = 4 if b_blocks > 1 else 0

    def spec(offset, advance):
        return pl.BlockSpec((chunk, ROWS, depth), lambda j, s, *_: (s, offset + advance * j, 0))

    return pl.pallas_call(
        correlate_kernel,
        grid_spec=pltpu.PrefetchScalarGridSpec(
            num_scalar_prefetch=1,
            grid=(b_blocks, blocks // chunk),
            in_specs=[spec(o, 0) for _, o in a_list]
            + [spec(o, stride) for _, o in b_list]
            + [pl.BlockSpec((2 * LAGS, freqs), lambda j, s, *_: (0, 0))],
            out_specs=[
                pl.BlockSpec((2, ROWS * b_count, LAGS), lambda j, s, *_: (0, j, 0)),
                pl.BlockSpec((2, b_count // 2 * a_count, LAGS), lambda j, s, *_: (0, j, 0)),
            ],
            scratch_shapes=[
                pltpu.VMEM((chunk, a_count, depth), jnp.float32),
                pltpu.VMEM((chunk, 2 * width, depth), jnp.bfloat16),
                pltpu.VMEM((freqs, a_count * width), jnp.bfloat16),
                pltpu.VMEM((b_count * a_count, LAGS), jnp.float32),
            ],
        ),
        out_shape=[
            jax.ShapeDtypeStruct((2, b_blocks * ROWS * b_count, LAGS), jnp.bfloat16),
            jax.ShapeDtypeStruct((2, b_blocks * b_count // 2 * a_count, LAGS), jnp.bfloat16),
        ],
        compiler_params=pltpu.CompilerParams(
            vmem_limit_bytes=VMEM_BYTES, dimension_semantics=("arbitrary", "arbitrary")
        ),
        name="correlate",
    )(order, *[a for a, _ in a_list], *[b for b, _ in b_list], table)


def whiten_sorted(raw, own, info):
    windows, width = raw.shape[1:]
    blocks = own.shape[0]

    def kernel(info_ref, raw_ref, own_ref, stay_ref, move_ref, wide_ref):
        low = pl.multiple_of(info_ref[2] * ROWS, ROWS)
        half_ref = raw_ref.at[pl.ds(low, ROWS)]

        @pl.when(info_ref[3] == 1)
        def _():
            stay_ref[...] = own_ref[...]
            whiten_block(half_ref, move_ref, wide_ref)

        @pl.when(info_ref[3] != 1)
        def _():
            move_ref[...] = own_ref[...]
            whiten_block(half_ref, stay_ref, wide_ref)

    shape = jax.ShapeDtypeStruct(own.shape, jnp.bfloat16)
    return pl.pallas_call(
        kernel,
        in_specs=[pl.BlockSpec(memory_space=pltpu.SMEM)] + [pl.BlockSpec(memory_space=pltpu.VMEM)] * 2,
        out_specs=[pl.BlockSpec(memory_space=pltpu.VMEM)] * 2,
        out_shape=[shape, shape],
        scratch_shapes=[pltpu.VMEM((blocks // windows * 2, ROWS * windows, windows * FINE), jnp.float32)],
        compiler_params=pltpu.CompilerParams(vmem_limit_bytes=VMEM_BYTES),
        name="whiten_sorted",
    )(info, raw, own)


def prepare(raw, partner, members):
    channels, windows, width = raw.shape
    blocks = width // 2 // FINE
    depth = 2 * windows * FINE
    count = partner.shape[0]
    chips = count // 2

    def kernel(partner_ref, raw_ref, rank_ref, info_ref, own_ref, moves_ref, half_ref, wide_ref, sem):
        group, member = lax.axis_index("group"), lax.axis_index("member")
        low = pl.multiple_of(group % 2 * ROWS, ROWS)
        copy = pltpu.make_async_copy(raw_ref.at[pl.ds(low, ROWS)], half_ref, sem)
        copy.start()
        for index in range(count):
            moves_ref[index] = -1
        for index in range(count):

            @pl.when(moves_ref[index] < 0)
            def _():
                def walk(_, here):
                    there = partner_ref[here]
                    moves_ref[here] = 0
                    moves_ref[there] = 1
                    return there ^ 1

                lax.fori_loop(0, chips, walk, jnp.int32(index))

        target = [partner_ref[2 * chip + 1 - moves_ref[2 * chip]] // 2 for chip in range(chips)]
        rank = jnp.int32(0)
        for i in range(chips):
            for j in range(i + 1, chips):
                rank += jnp.where(target[j] < target[i], math.factorial(chips - 1 - i), 0)
        rank_ref[0] = rank
        info_ref[0] = jnp.where(member < members // 2, 1, 0)
        info_ref[1] = member % 2
        info_ref[2] = group % 2
        info_ref[3] = 1 - moves_ref[group]
        copy.wait()
        whiten_block(half_ref, own_ref, wide_ref)

    return pl.pallas_call(
        kernel,
        in_specs=[pl.BlockSpec(memory_space=pltpu.SMEM), pl.BlockSpec(memory_space=pl.ANY)],
        out_specs=[pl.BlockSpec(memory_space=pltpu.SMEM)] * 2 + [pl.BlockSpec(memory_space=pltpu.VMEM)],
        out_shape=[
            jax.ShapeDtypeStruct((1,), jnp.int32),
            jax.ShapeDtypeStruct((4,), jnp.int32),
            jax.ShapeDtypeStruct((blocks, ROWS, depth), jnp.bfloat16),
        ],
        scratch_shapes=[
            pltpu.SMEM((count,), jnp.int32),
            pltpu.VMEM((ROWS, windows, width), jnp.bfloat16),
            pltpu.VMEM((blocks // windows * 2, ROWS * windows, windows * FINE), jnp.float32),
            pltpu.SemaphoreType.DMA(()),
        ],
        compiler_params=pltpu.CompilerParams(vmem_limit_bytes=VMEM_BYTES),
        name="prepare",
    )(pltpu.with_memory_space_constraint(partner, pltpu.HBM), pltpu.with_memory_space_constraint(raw, pltpu.HBM))


def choose(info, pieces):
    shape = pieces[0].shape

    def kernel(info_ref, far_ref, near_ref, here_ref, there_ref, out_ref, sems):
        def run(first, second):
            copies = [
                pltpu.make_async_copy(ref, out_ref.at[index], sems.at[index])
                for index, ref in enumerate((first, second))
            ]
            for copy in copies:
                copy.start()
            for copy in copies:
                copy.wait()

        @pl.when(info_ref[3] == 1)
        def _():
            run(here_ref, there_ref)

        @pl.when(info_ref[3] != 1)
        def _():
            run(far_ref, near_ref)

    return pl.pallas_call(
        kernel,
        in_specs=[pl.BlockSpec(memory_space=pltpu.SMEM)] + [pl.BlockSpec(memory_space=pl.ANY)] * 4,
        out_specs=pl.BlockSpec(memory_space=pltpu.VMEM),
        out_shape=jax.ShapeDtypeStruct((2,) + shape, jnp.bfloat16),
        scratch_shapes=[pltpu.SemaphoreType.DMA((2,))],
        compiler_params=pltpu.CompilerParams(vmem_limit_bytes=VMEM_BYTES),
        name="choose",
    )(info, *pieces)


def place(info, pieces, members, whole=None):
    others = 2 * members * ROWS
    half = others // 2
    rest = () if whole is None else (whole,)

    def kernel(info_ref, *refs):
        out_ref, sems = refs[-2:]
        odd, core = info_ref[1], info_ref[2]
        if whole is None:
            which = core
            far_ref, near_ref, here_ref, there_ref = refs[:4]
        else:
            which = 1 - core
            far_ref, near_ref = here_ref, there_ref = refs[0].at[0], refs[0].at[1]

        def run(copies):
            copies = [pltpu.make_async_copy(*copy, sems.at[index]) for index, copy in enumerate(copies)]
            for copy in copies:
                copy.start()
            for copy in copies:
                copy.wait()

        def put_stay(side, ref):
            low = pl.multiple_of(which * ROWS, ROWS)
            at = pl.multiple_of(side * half, half)
            return [(ref.reshape(ROWS, half, LAGS), out_ref.at[pl.ds(low, ROWS), pl.ds(at, half), :])]

        def put_move(side, ref):
            source = ref.reshape(2 * ROWS, 2 * ROWS, LAGS)
            copies = []
            for shard in range(2):
                at = pl.multiple_of(side * half + shard * 2 * ROWS + which * ROWS, ROWS)
                copies.append((source.at[:, pl.ds(shard * ROWS, ROWS), :], out_ref.at[:, pl.ds(at, ROWS), :]))
            return copies

        @pl.when(info_ref[3] == 1)
        def _():
            run(put_stay(1 - odd, far_ref) + put_stay(odd, near_ref))

        @pl.when(info_ref[3] != 1)
        def _():
            run(put_move(odd, here_ref) + put_move(1 - odd, there_ref))

    return pl.pallas_call(
        kernel,
        in_specs=[pl.BlockSpec(memory_space=pltpu.SMEM)]
        + [pl.BlockSpec(memory_space=pltpu.VMEM)] * len(pieces)
        + [pl.BlockSpec(memory_space=pl.ANY)] * len(rest),
        out_specs=pl.BlockSpec(memory_space=pl.ANY),
        out_shape=jax.ShapeDtypeStruct((2 * ROWS, others, LAGS), jnp.bfloat16),
        scratch_shapes=[pltpu.SemaphoreType.DMA((4,))],
        input_output_aliases={1 + len(pieces): 0} if rest else {},
        compiler_params=pltpu.CompilerParams(vmem_limit_bytes=VMEM_BYTES),
        name="place",
    )(info, *pieces, *rest)


def permute(value, groups, members, target):
    pairs = []
    for group, member in itertools.product(range(groups), range(members)):
        to_group, to_member = target(group, member)
        pairs.append((group * members + member, to_group * members + to_member))
    return lax.ppermute(value, ("group", "member"), pairs)


def on_device_any(spectra, partner):
    group_count = lax.axis_size("group")
    channels, windows, width = spectra.shape
    white = whiten(spectra)
    blocks, _, depth = white.shape
    spread = lax.all_to_all(white, "group", split_axis=1, concat_axis=1, tiled=True)
    shares = spread.reshape(blocks, group_count, channels // group_count, depth)
    ordered = jnp.take(shares, partner, axis=1).reshape(white.shape)
    arrived = lax.all_to_all(ordered, "group", split_axis=1, concat_axis=1, tiled=True)
    theirs = lax.all_gather(arrived, "member", axis=1, tiled=True)
    table = jnp.asarray(lag_rows(width // 2, windows))
    others = theirs.shape[1]
    order = jnp.zeros((3,), jnp.int32)
    result, _ = correlate(
        order, [(white, 0), (white, 1)], [(theirs, q) for q in range(4)], table, others // (4 * ROWS)
    )
    result = result.reshape(2, others // (4 * ROWS), ROWS, 4 * ROWS, LAGS)
    return jnp.transpose(result, (0, 2, 1, 3, 4)).reshape(channels, others, LAGS)


def on_device_pairs(spectra, partner):
    groups, members = lax.axis_size("group"), lax.axis_size("member")
    chips = groups // 2
    windows, width = spectra.shape[1:]

    def across(value):
        return permute(value, groups, members, lambda g, m: (g ^ 1, m))

    other_raw = across(spectra)
    rank, info, own = prepare(spectra, partner, members)
    stay, move = whiten_sorted(other_raw, own, info)

    far = (2, 0, 3, 1)
    back = tuple(far.index(m) for m in range(members))
    near = (0, 2, 1, 3)
    orders = list(itertools.permutations(range(chips)))

    def straight_way(order):
        return sum(order[chip] == chips - 1 - chip for chip in range(chips)) < 2

    def go(order):
        def branch(stay, move):
            def go_on(value, flip):
                return permute(value, groups, members, lambda g, m: (2 * order[g // 2] + g % 2, m ^ flip))

            here = go_on(move, 0)
            first = permute(stay, groups, members, lambda g, m: (g, far[m]))
            if straight_way(order):
                there = go_on(move, 1)
            else:
                there = permute(here, groups, members, lambda g, m: (g, m ^ 1))
                _, stay = lax.optimization_barrier((first, stay))
            second = permute(stay, groups, members, lambda g, m: (g, near[m]))
            return first, second, here, across(here), there, across(there)

        return branch

    def home(order):
        def branch(first, second, same, other):
            def back_home(value, flip):
                return permute(value, groups, members, lambda g, m: (2 * order.index(g // 2) + g % 2, m ^ flip))

            here = back_home(same, 0)
            from_near = permute(second, groups, members, lambda g, m: (g, near[m]))
            if straight_way(order):
                there = back_home(other, 1)
            else:
                swapped = permute(other, groups, members, lambda g, m: (g, m ^ 1))
                first, swapped, _, _ = lax.optimization_barrier((first, swapped, from_near, here))
                there = back_home(swapped, 0)
            from_far = permute(first, groups, members, lambda g, m: (g, back[m]))
            return from_far, from_near, here, there

        return branch

    first, second, here, here_too, there, there_too = lax.switch(
        rank[0], [go(order) for order in orders], stay, move
    )
    table = jnp.asarray(lag_rows(width // 2, windows))
    straight, mirrored = correlate(
        info,
        [(first, 0), (second, 0)],
        [(here, 0), (here_too, 0), (there, 0), (there_too, 0)],
        table,
        1,
    )
    pieces = lax.switch(
        rank[0], [home(order) for order in orders], straight[0], straight[1], mirrored[0], mirrored[1]
    )
    got = across(choose(info, pieces))
    return place(info, (got,), members, place(info, pieces, members))


def solution(mesh):
    placed = (P(("group", "member"), None, None), P())
    small = mesh.shape["group"] <= 8 and mesh.shape["member"] == 4
    return jax.shard_map(
        on_device_pairs if small else on_device_any,
        mesh=mesh,
        in_specs=placed,
        out_specs=P(("group", "member"), None, None),
        check_vma=False,
    )
```

```python
import itertools
import math

import jax
import jax.numpy as jnp
import ml_dtypes
import numpy as np
from jax import lax
from jax.experimental import pallas as pl
from jax.experimental.pallas import tpu as pltpu
from jax.sharding import PartitionSpec as P

LAGS = 128
HALF = 64
FINE = 16
ROWS = 16
VMEM_BYTES = 48 * 1024 * 1024


def lag_rows(freq_count, window_count):
    lag = np.arange(LAGS) - LAGS // 2
    freq = np.arange(freq_count)
    angle = np.pi * np.mod(lag[:, None] * freq[None, :], 2 * freq_count) / freq_count
    norm = 1.0 / math.sqrt(window_count * freq_count)
    rows = np.concatenate([np.cos(angle), -np.sin(angle)], axis=0) * norm
    return rows.astype(np.float32).astype(ml_dtypes.bfloat16)


def whiten_block(raw_ref, out_ref, wide_ref):
    rows, windows, width = raw_ref.shape
    freqs = width // 2
    lanes = windows * FINE
    groups = freqs // lanes
    for slab in range(2 * groups):
        value = raw_ref[:, :, slab * lanes : (slab + 1) * lanes].astype(jnp.float32)
        wide_ref[slab] = value.reshape(rows * windows, lanes)

    def window(slab, w):
        return wide_ref[slab, pl.ds(w, rows, stride=windows), :]

    pieces = []
    for group in range(groups):
        piece = jnp.zeros((rows, lanes), jnp.float32)
        for w in range(windows):
            real, imag = window(group, w), window(groups + group, w)
            piece += real * real + imag * imag
        pieces.append(piece)
    power = jnp.concatenate(pieces, axis=1)
    edge = jnp.zeros((rows, 2 * HALF), jnp.float32)
    padded = jnp.concatenate([edge, power, edge], axis=1)
    total = padded
    length = padded.shape[1]
    step = 1
    while step < 2 * HALF:
        total = total + pltpu.roll(total, length - step, axis=1)
        step *= 2
    total = total + pltpu.roll(padded, length - 2 * HALF, axis=1)
    smoothed = pltpu.roll(total, length - HALF, axis=1)[:, :freqs]
    place = lax.broadcasted_iota(jnp.int32, (rows, freqs), 1)
    counts = jnp.minimum(place + HALF, freqs - 1) - jnp.maximum(place - HALF, 0) + 1
    average = smoothed / (counts.astype(jnp.float32) * windows)
    factor = 1.0 / jnp.sqrt(average + 1e-05)
    granule = lax.broadcasted_iota(jnp.int32, (rows, lanes), 1) // FINE
    for part in range(2):
        for group in range(groups):
            scale = factor[:, group * lanes : (group + 1) * lanes]
            items = [window(part * groups + group, w) * scale for w in range(windows)]
            dist = windows // 2
            while dist:
                keep = (granule & dist) == 0
                nxt = list(items)
                for i in range(windows):
                    if i & dist:
                        continue
                    j = i + dist
                    nxt[i] = jnp.where(keep, items[i], pltpu.roll(items[j], dist * FINE, axis=1))
                    nxt[j] = jnp.where(keep, pltpu.roll(items[i], lanes - dist * FINE, axis=1), items[j])
                items = nxt
                dist //= 2
            for i in range(windows):
                out_ref[group * windows + i, :, part * lanes : (part + 1) * lanes] = items[i].astype(jnp.bfloat16)


def whiten(raw):
    channels, windows, width = raw.shape
    blocks = width // 2 // FINE
    return pl.pallas_call(
        whiten_block,
        grid=(channels // ROWS,),
        in_specs=[pl.BlockSpec((ROWS, windows, width), lambda i: (i, 0, 0))],
        out_specs=pl.BlockSpec((blocks, ROWS, 2 * windows * FINE), lambda i: (0, i, 0)),
        out_shape=jax.ShapeDtypeStruct((blocks, channels, 2 * windows * FINE), jnp.bfloat16),
        scratch_shapes=[pltpu.VMEM((blocks // windows * 2, ROWS * windows, windows * FINE), jnp.float32)],
        compiler_params=pltpu.CompilerParams(vmem_limit_bytes=VMEM_BYTES),
        name="whiten",
    )(raw)


def correlate_kernel(order_ref, a1, a2, b1, b2, b3, b4, table_ref, own_ref, other_ref, rows_ref, rhs_ref, cross_ref, flip_ref):
    step = pl.program_id(1)
    chunk, _, depth = a1.shape
    half = depth // 2
    a_count = 2 * ROWS
    b_count = 4 * ROWS
    width = 2 * b_count
    swap_a, swap_b, first_half = order_ref[0], order_ref[1], order_ref[2]
    part = FINE // 2
    lane = lax.broadcasted_iota(jnp.int32, (part, depth), 1)
    mask = (lane % part == lax.broadcasted_iota(jnp.int32, (part, depth), 0)).astype(jnp.float32)
    upper = (lax.broadcasted_iota(jnp.int32, (ROWS, depth), 1) // part % 2).astype(jnp.float32)
    upper = upper.astype(jnp.bfloat16)
    sides = (1 - upper, upper)

    for index, ref in enumerate((a1, a2)):
        at = pl.multiple_of((index ^ swap_a) * ROWS, ROWS)
        for f in range(chunk):
            rows_ref[f, pl.ds(at, ROWS), :] = ref[f].astype(jnp.float32)
    for index, ref in enumerate((b1, b2, b3, b4)):
        spot = ((index // 2) ^ swap_b) * 2 + ((index % 2) ^ first_half)
        at = pl.multiple_of(spot * ROWS, ROWS)
        for f in range(chunk):
            value = ref[f]
            turned = jnp.concatenate([-value[:, half:], value[:, :half]], axis=1)
            for side in range(2):
                rhs_ref[f, pl.ds(side * width + at, ROWS), :] = value * sides[side]
                rhs_ref[f, pl.ds(side * width + b_count + at, ROWS), :] = turned * sides[side]
    for f in range(chunk):
        parts = []
        for i in range(a_count):
            parts.append(jnp.broadcast_to(rows_ref[f, i : i + 1, :], (part, depth)) * mask)
        left = jnp.concatenate(parts, axis=0).astype(jnp.bfloat16)
        cross = lax.dot_general(
            left, rhs_ref[f], (((1,), (1,)), ((), ())), preferred_element_type=jnp.float32
        )
        at = pl.multiple_of((step * chunk + f) * FINE, FINE)
        for i in range(a_count):
            rows = cross[i * part : (i + 1) * part]
            both = jnp.concatenate([rows[:, :width], rows[:, width:]], axis=0)
            cross_ref[pl.ds(at, FINE), i * width : (i + 1) * width] = both.astype(jnp.bfloat16)

    @pl.when(step == pl.num_programs(1) - 1)
    def _():
        low = lax.broadcasted_iota(jnp.int32, (LAGS, width), 1) < b_count
        for pair in range(a_count // 2):
            wide = jnp.dot(
                table_ref[...], cross_ref[:, 2 * pair * width : 2 * (pair + 1) * width], preferred_element_type=jnp.float32
            )
            for i in (2 * pair, 2 * pair + 1):
                both = wide[:, (i % 2) * width : (i % 2 + 1) * width]
                cos_part, sin_part = both[:LAGS], both[LAGS:]
                joined = jnp.where(
                    low,
                    cos_part + pltpu.roll(sin_part, b_count, axis=1),
                    pltpu.roll(cos_part, b_count, axis=1) - sin_part,
                )
                turned = joined.T
                at = i % ROWS * b_count
                own_ref[(i // ROWS) ^ swap_a, at : at + b_count, :] = turned[:b_count].astype(jnp.bfloat16)
                flip_ref[pl.ds(i, b_count, stride=a_count), :] = turned[b_count:]
        span = b_count // 2 * a_count
        for index in range(2):
            value = flip_ref[index * span : (index + 1) * span, :].astype(jnp.bfloat16)
            other_ref[index ^ swap_b] = value


def correlate(order, a_list, b_list, table, b_blocks, chunk=32):
    blocks, _, depth = a_list[0][0].shape
    freqs = blocks * FINE
    a_count, b_count = 2 * ROWS, 4 * ROWS
    width = 2 * b_count
    stride = 4 if b_blocks > 1 else 0

    def spec(offset, advance):
        return pl.BlockSpec((chunk, ROWS, depth), lambda j, s, *_: (s, offset + advance * j, 0))

    return pl.pallas_call(
        correlate_kernel,
        grid_spec=pltpu.PrefetchScalarGridSpec(
            num_scalar_prefetch=1,
            grid=(b_blocks, blocks // chunk),
            in_specs=[spec(o, 0) for _, o in a_list]
            + [spec(o, stride) for _, o in b_list]
            + [pl.BlockSpec((2 * LAGS, freqs), lambda j, s, *_: (0, 0))],
            out_specs=[
                pl.BlockSpec((2, ROWS * b_count, LAGS), lambda j, s, *_: (0, j, 0)),
                pl.BlockSpec((2, b_count // 2 * a_count, LAGS), lambda j, s, *_: (0, j, 0)),
            ],
            scratch_shapes=[
                pltpu.VMEM((chunk, a_count, depth), jnp.float32),
                pltpu.VMEM((chunk, 2 * width, depth), jnp.bfloat16),
                pltpu.VMEM((freqs, a_count * width), jnp.bfloat16),
                pltpu.VMEM((b_count * a_count, LAGS), jnp.float32),
            ],
        ),
        out_shape=[
            jax.ShapeDtypeStruct((2, b_blocks * ROWS * b_count, LAGS), jnp.bfloat16),
            jax.ShapeDtypeStruct((2, b_blocks * b_count // 2 * a_count, LAGS), jnp.bfloat16),
        ],
        compiler_params=pltpu.CompilerParams(
            vmem_limit_bytes=VMEM_BYTES, dimension_semantics=("arbitrary", "arbitrary")
        ),
        name="correlate",
    )(order, *[a for a, _ in a_list], *[b for b, _ in b_list], table)


def whiten_sorted(raw, own, info):
    windows, width = raw.shape[1:]
    blocks = own.shape[0]

    def kernel(info_ref, raw_ref, own_ref, stay_ref, move_ref, wide_ref):
        low = pl.multiple_of(info_ref[2] * ROWS, ROWS)
        half_ref = raw_ref.at[pl.ds(low, ROWS)]

        @pl.when(info_ref[3] == 1)
        def _():
            stay_ref[...] = own_ref[...]
            whiten_block(half_ref, move_ref, wide_ref)

        @pl.when(info_ref[3] != 1)
        def _():
            move_ref[...] = own_ref[...]
            whiten_block(half_ref, stay_ref, wide_ref)

    shape = jax.ShapeDtypeStruct(own.shape, jnp.bfloat16)
    return pl.pallas_call(
        kernel,
        in_specs=[pl.BlockSpec(memory_space=pltpu.SMEM)] + [pl.BlockSpec(memory_space=pltpu.VMEM)] * 2,
        out_specs=[pl.BlockSpec(memory_space=pltpu.VMEM)] * 2,
        out_shape=[shape, shape],
        scratch_shapes=[pltpu.VMEM((blocks // windows * 2, ROWS * windows, windows * FINE), jnp.float32)],
        compiler_params=pltpu.CompilerParams(vmem_limit_bytes=VMEM_BYTES),
        name="whiten_sorted",
    )(info, raw, own)


def prepare(raw, partner, members):
    channels, windows, width = raw.shape
    blocks = width // 2 // FINE
    depth = 2 * windows * FINE
    count = partner.shape[0]
    chips = count // 2

    def kernel(partner_ref, raw_ref, rank_ref, info_ref, own_ref, moves_ref, half_ref, wide_ref, sem):
        group, member = lax.axis_index("group"), lax.axis_index("member")
        low = pl.multiple_of(group % 2 * ROWS, ROWS)
        copy = pltpu.make_async_copy(raw_ref.at[pl.ds(low, ROWS)], half_ref, sem)
        copy.start()
        for index in range(count):
            moves_ref[index] = -1
        for index in range(count):

            @pl.when(moves_ref[index] < 0)
            def _():
                def walk(_, here):
                    there = partner_ref[here]
                    moves_ref[here] = 0
                    moves_ref[there] = 1
                    return there ^ 1

                lax.fori_loop(0, chips, walk, jnp.int32(index))

        target = [partner_ref[2 * chip + 1 - moves_ref[2 * chip]] // 2 for chip in range(chips)]
        rank = jnp.int32(0)
        for i in range(chips):
            for j in range(i + 1, chips):
                rank += jnp.where(target[j] < target[i], math.factorial(chips - 1 - i), 0)
        rank_ref[0] = rank
        info_ref[0] = jnp.where(member < members // 2, 1, 0)
        info_ref[1] = member % 2
        info_ref[2] = group % 2
        info_ref[3] = 1 - moves_ref[group]
        copy.wait()
        whiten_block(half_ref, own_ref, wide_ref)

    return pl.pallas_call(
        kernel,
        in_specs=[pl.BlockSpec(memory_space=pltpu.SMEM), pl.BlockSpec(memory_space=pl.ANY)],
        out_specs=[pl.BlockSpec(memory_space=pltpu.SMEM)] * 2 + [pl.BlockSpec(memory_space=pltpu.VMEM)],
        out_shape=[
            jax.ShapeDtypeStruct((1,), jnp.int32),
            jax.ShapeDtypeStruct((4,), jnp.int32),
            jax.ShapeDtypeStruct((blocks, ROWS, depth), jnp.bfloat16),
        ],
        scratch_shapes=[
            pltpu.SMEM((count,), jnp.int32),
            pltpu.VMEM((ROWS, windows, width), jnp.bfloat16),
            pltpu.VMEM((blocks // windows * 2, ROWS * windows, windows * FINE), jnp.float32),
            pltpu.SemaphoreType.DMA(()),
        ],
        compiler_params=pltpu.CompilerParams(vmem_limit_bytes=VMEM_BYTES),
        name="prepare",
    )(pltpu.with_memory_space_constraint(partner, pltpu.HBM), pltpu.with_memory_space_constraint(raw, pltpu.HBM))


def choose(info, pieces):
    shape = pieces[0].shape

    def kernel(info_ref, far_ref, near_ref, here_ref, there_ref, out_ref, sems):
        def run(first, second):
            copies = [
                pltpu.make_async_copy(ref, out_ref.at[index], sems.at[index])
                for index, ref in enumerate((first, second))
            ]
            for copy in copies:
                copy.start()
            for copy in copies:
                copy.wait()

        @pl.when(info_ref[3] == 1)
        def _():
            run(here_ref, there_ref)

        @pl.when(info_ref[3] != 1)
        def _():
            run(far_ref, near_ref)

    return pl.pallas_call(
        kernel,
        in_specs=[pl.BlockSpec(memory_space=pltpu.SMEM)] + [pl.BlockSpec(memory_space=pl.ANY)] * 4,
        out_specs=pl.BlockSpec(memory_space=pltpu.VMEM),
        out_shape=jax.ShapeDtypeStruct((2,) + shape, jnp.bfloat16),
        scratch_shapes=[pltpu.SemaphoreType.DMA((2,))],
        compiler_params=pltpu.CompilerParams(vmem_limit_bytes=VMEM_BYTES),
        name="choose",
    )(info, *pieces)


def place(info, pieces, members, whole=None):
    others = 2 * members * ROWS
    half = others // 2
    rest = () if whole is None else (whole,)

    def kernel(info_ref, *refs):
        out_ref, sems = refs[-2:]
        odd, core = info_ref[1], info_ref[2]
        if whole is None:
            which = core
            far_ref, near_ref, here_ref, there_ref = refs[:4]
        else:
            which = 1 - core
            far_ref, near_ref = here_ref, there_ref = refs[0].at[0], refs[0].at[1]

        def run(copies):
            copies = [pltpu.make_async_copy(*copy, sems.at[index]) for index, copy in enumerate(copies)]
            for copy in copies:
                copy.start()
            for copy in copies:
                copy.wait()

        def put_stay(side, ref):
            low = pl.multiple_of(which * ROWS, ROWS)
            at = pl.multiple_of(side * half, half)
            return [(ref.reshape(ROWS, half, LAGS), out_ref.at[pl.ds(low, ROWS), pl.ds(at, half), :])]

        def put_move(side, ref):
            source = ref.reshape(2 * ROWS, 2 * ROWS, LAGS)
            copies = []
            for shard in range(2):
                at = pl.multiple_of(side * half + shard * 2 * ROWS + which * ROWS, ROWS)
                copies.append((source.at[:, pl.ds(shard * ROWS, ROWS), :], out_ref.at[:, pl.ds(at, ROWS), :]))
            return copies

        @pl.when(info_ref[3] == 1)
        def _():
            run(put_stay(1 - odd, far_ref) + put_stay(odd, near_ref))

        @pl.when(info_ref[3] != 1)
        def _():
            run(put_move(odd, here_ref) + put_move(1 - odd, there_ref))

    return pl.pallas_call(
        kernel,
        in_specs=[pl.BlockSpec(memory_space=pltpu.SMEM)]
        + [pl.BlockSpec(memory_space=pltpu.VMEM)] * len(pieces)
        + [pl.BlockSpec(memory_space=pl.ANY)] * len(rest),
        out_specs=pl.BlockSpec(memory_space=pl.ANY),
        out_shape=jax.ShapeDtypeStruct((2 * ROWS, others, LAGS), jnp.bfloat16),
        scratch_shapes=[pltpu.SemaphoreType.DMA((4,))],
        input_output_aliases={1 + len(pieces): 0} if rest else {},
        compiler_params=pltpu.CompilerParams(vmem_limit_bytes=VMEM_BYTES),
        name="place",
    )(info, *pieces, *rest)


def permute(value, groups, members, target):
    pairs = []
    for group, member in itertools.product(range(groups), range(members)):
        to_group, to_member = target(group, member)
        pairs.append((group * members + member, to_group * members + to_member))
    return lax.ppermute(value, ("group", "member"), pairs)


def on_device_any(spectra, partner):
    group_count = lax.axis_size("group")
    channels, windows, width = spectra.shape
    white = whiten(spectra)
    blocks, _, depth = white.shape
    spread = lax.all_to_all(white, "group", split_axis=1, concat_axis=1, tiled=True)
    shares = spread.reshape(blocks, group_count, channels // group_count, depth)
    ordered = jnp.take(shares, partner, axis=1).reshape(white.shape)
    arrived = lax.all_to_all(ordered, "group", split_axis=1, concat_axis=1, tiled=True)
    theirs = lax.all_gather(arrived, "member", axis=1, tiled=True)
    table = jnp.asarray(lag_rows(width // 2, windows))
    others = theirs.shape[1]
    order = jnp.zeros((3,), jnp.int32)
    result, _ = correlate(
        order, [(white, 0), (white, 1)], [(theirs, q) for q in range(4)], table, others // (4 * ROWS)
    )
    result = result.reshape(2, others // (4 * ROWS), ROWS, 4 * ROWS, LAGS)
    return jnp.transpose(result, (0, 2, 1, 3, 4)).reshape(channels, others, LAGS)


def on_device_pairs(spectra, partner):
    groups, members = lax.axis_size("group"), lax.axis_size("member")
    chips = groups // 2
    windows, width = spectra.shape[1:]

    def across(value):
        return permute(value, groups, members, lambda g, m: (g ^ 1, m))

    other_raw = across(spectra)
    rank, info, own = prepare(spectra, partner, members)
    stay, move = whiten_sorted(other_raw, own, info)

    far = (2, 0, 3, 1)
    back = tuple(far.index(m) for m in range(members))
    near = (0, 2, 1, 3)
    orders = list(itertools.permutations(range(chips)))

    def straight_way(order):
        moving = sum(order[chip] != chip for chip in range(chips))
        return moving <= 2 or sum(order[chip] == chips - 1 - chip for chip in range(chips)) < 2

    def go(order):
        def branch(stay, move):
            def go_on(value, flip):
                return permute(value, groups, members, lambda g, m: (2 * order[g // 2] + g % 2, m ^ flip))

            here = go_on(move, 0)
            first = permute(stay, groups, members, lambda g, m: (g, far[m]))
            if straight_way(order):
                there = go_on(move, 1)
            else:
                there = permute(here, groups, members, lambda g, m: (g, m ^ 1))
                _, stay = lax.optimization_barrier((first, stay))
            second = permute(stay, groups, members, lambda g, m: (g, near[m]))
            return first, second, here, across(here), there, across(there)

        return branch

    def home(order):
        def branch(first, second, same, other):
            def back_home(value, flip):
                return permute(value, groups, members, lambda g, m: (2 * order.index(g // 2) + g % 2, m ^ flip))

            here = back_home(same, 0)
            from_near = permute(second, groups, members, lambda g, m: (g, near[m]))
            if straight_way(order):
                there = back_home(other, 1)
            else:
                swapped = permute(other, groups, members, lambda g, m: (g, m ^ 1))
                first, swapped, _, _ = lax.optimization_barrier((first, swapped, from_near, here))
                there = back_home(swapped, 0)
            from_far = permute(first, groups, members, lambda g, m: (g, back[m]))
            return from_far, from_near, here, there

        return branch

    first, second, here, here_too, there, there_too = lax.switch(
        rank[0], [go(order) for order in orders], stay, move
    )
    table = jnp.asarray(lag_rows(width // 2, windows))
    straight, mirrored = correlate(
        info,
        [(first, 0), (second, 0)],
        [(here, 0), (here_too, 0), (there, 0), (there_too, 0)],
        table,
        1,
    )
    pieces = lax.switch(
        rank[0], [home(order) for order in orders], straight[0], straight[1], mirrored[0], mirrored[1]
    )
    got = across(choose(info, pieces))
    return place(info, (got,), members, place(info, pieces, members))


def solution(mesh):
    placed = (P(("group", "member"), None, None), P())
    small = mesh.shape["group"] <= 8 and mesh.shape["member"] == 4
    return jax.shard_map(
        on_device_pairs if small else on_device_any,
        mesh=mesh,
        in_specs=placed,
        out_specs=P(("group", "member"), None, None),
        check_vma=False,
    )
```
